256 devices in a mesh: row: 8 (over x, core), col: 32 (over y, z).
Axes of the slice: x: 4, y: 4, z: 8, core: 2. Of those that a mesh axis runs over, the one named last changes fastest.
Arguments:
- strand_layout: float32 [7, 131072], P(None, ('row', 'col')), may hold values from -0.0034938562 to 1, as said below
- strand_amperes_panel: float32 [16, 131072], P(None, ('row', 'col')), may hold values from -7 to 7
- krylov_vectors: float32 [64, 131072], P(None, ('row', 'col')), may hold values from -0.015625 to 0.015625
- strand_kelvin: float32 [131072], P(('row', 'col')), may hold values from 1.9 to 10
- strand_ohmic_value: float32 [131072], P(('row', 'col')), may hold values from 0.2 to 1
- strand_warmer_slot: int32 [131072], P(('row', 'col')), may hold values from 0 to 7
- warmer_kelvin_gain: float32 [8], replicated, may hold values from 0 to 6
- strand_region_slot: int32 [131072], P(('row', 'col')), may hold values from 0 to 31
- region_threshold_kelvin: float32 [32], replicated, may hold values from 5 to 12
Outputs:
- q_next: float32 [16, 131072], P(None, ('row', 'col'))
- hess: float32 [64, 16], replicated
- chol: float32 [16, 16], replicated
- joule: float32 [131072], P(('row', 'col'))
The draws below stay inside these ranges and needn't reach their ends.
Inputs may be any that keep to these rules, and one draw needn't show every extreme that they name: `strand_layout`: rows 0-2 lie in the unit cube, rows 3-5 within -0.4 * sqrt(10 / 131072) to sqrt(10 / 131072), row 6 in 0.005 to 0.05.
All inputs are finite; a program needn't handle non-finite values.
Results may differ from the reference program's by a relative error of at most 0.0007.
Values may be sent and summed in bfloat16 or wider, within the bound.
No kernel may reach another device: no remote copies, remote signals or barrier semaphores. Data moves between devices by JAX's collectives and lax.ppermute only.
A program may use at most 64 MiB of HBM per device.

```python
import math
import jax
import jax.numpy as jnp
from jax import lax

SECTIONS = 16
BASIS = 64
WARMING_LOOPS = 8
QUENCH_AREAS = 32
STRAND_COUNT = 131072


seg_gain = 10.0


def centres(key):
    spots = jax.random.uniform(jax.random.fold_in(key, 101), (3, STRAND_COUNT), jnp.float32)
    return spots


def draw_strand_layout(key, part):
    spots = centres(key)
    key_along, key_across, key_rad = jax.random.split(jax.random.fold_in(key, 303), 3)
    length = jnp.float32(math.sqrt(seg_gain / STRAND_COUNT))
    along = jax.random.uniform(key_along, (1, STRAND_COUNT), jnp.float32, minval=0.6, maxval=1.0)
    across = jax.random.uniform(key_across, (2, STRAND_COUNT), jnp.float32, minval=-0.4, maxval=0.4)
    segment = length * jnp.concatenate([across, along], axis=0)
    radius = jnp.exp(jax.random.uniform(key_rad, (1, STRAND_COUNT), jnp.float32, minval=math.log(0.005), maxval=math.log(0.05)))
    return jnp.concatenate([spots, segment, radius], axis=0)


def draw_strand_amperes_panel(key, part):
    spots = centres(key)
    key_flat, key_tall, key_phase, key_rough = jax.random.split(jax.random.fold_in(key, 202), 4)
    flat_waves = jax.random.randint(key_flat, (SECTIONS, 2), 0, 3).astype(jnp.float32)
    tall_waves = jax.random.randint(key_tall, (SECTIONS, 1), 1, 3).astype(jnp.float32)
    phase = jax.random.uniform(key_phase, (SECTIONS, 1), jnp.float32, minval=-math.pi, maxval=math.pi)
    angle = flat_waves[:, 0:1] * spots[0:1] + flat_waves[:, 1:2] * spots[1:2] + tall_waves * spots[2:3]
    smooth = jnp.cos(2.0 * math.pi * angle + phase)
    rough = jax.random.truncated_normal(key_rough, -5.0, 5.0, (SECTIONS, STRAND_COUNT), jnp.float32)
    return smooth + rough


def with_ends(values, stream_key, least, high):
    spot = [jax.random.randint(jax.random.fold_in(stream_key, axis), (), 0, length) for axis, length in enumerate(values.shape)]
    longest = values.shape.index(max(values.shape))
    next_to = spot[:longest] + [(spot[longest] + 1) % values.shape[longest]] + spot[longest + 1:]
    return values.at[tuple(spot)].set(least).at[tuple(next_to)].set(high)


def shard_levels(own_key, dims, shards, least, largest):
    loudness, own = 1.0, jax.random.fold_in(own_key, 6)
    for dim, blocks in shards:
        draws = jnp.exp(jax.random.uniform(jax.random.fold_in(own, dim), (blocks,), jnp.float32, least / len(shards), largest / len(shards)))
        loudness = loudness * jnp.repeat(draws, dims[dim] // blocks).reshape([-1 if axis == dim else 1 for axis in range(len(dims))])
    return loudness


def noise(own_key, shape, scale, most, cuts=(), kind=jnp.bfloat16):
    values = scale * jax.random.normal(own_key, shape, jnp.float32)
    if cuts:
        values = values * shard_levels(own_key, shape, cuts, -0.22, 0.18)
    return jnp.clip(values, -most, most).astype(kind)


def setup_inputs(seed: int = 0) -> dict:
    arg_keys = jax.random.split(jax.random.key(seed), 10)
    return {
        "strand_layout": draw_strand_layout(jax.random.fold_in(arg_keys[9], 71), 0),
        "strand_amperes_panel": draw_strand_amperes_panel(jax.random.fold_in(arg_keys[9], 71), 0),
        "krylov_vectors": noise(arg_keys[2], (BASIS, STRAND_COUNT), STRAND_COUNT ** -0.5, 0.015625, ((1, 256),), jnp.float32),
        "strand_kelvin": jnp.clip(1.9 + 8.1 * jax.random.uniform(arg_keys[3], (STRAND_COUNT,), jnp.float32) ** shard_levels(arg_keys[3], (STRAND_COUNT,), ((0, 256),), -0.2, 0.2), 1.9, 10.0),
        "strand_ohmic_value": jnp.clip(jnp.exp(math.log(1.0) - 1.609438 * jax.random.uniform(arg_keys[4], (STRAND_COUNT,), jnp.float32) ** shard_levels(arg_keys[4], (STRAND_COUNT,), ((0, 256),), -0.2, 0.2)), 0.2, 1.0),
        "strand_warmer_slot": with_ends(jax.random.randint(arg_keys[5], (STRAND_COUNT,), 0, WARMING_LOOPS), jax.random.fold_in(arg_keys[5], 1), 0, WARMING_LOOPS - 1).astype(jnp.int32),
        "warmer_kelvin_gain": jnp.clip(jax.random.uniform(arg_keys[6], (WARMING_LOOPS,), jnp.float32, 0.0, 6.0), 0.0, 6.0),
        "strand_region_slot": with_ends(jax.random.randint(arg_keys[7], (STRAND_COUNT,), 0, QUENCH_AREAS), jax.random.fold_in(arg_keys[7], 1), 0, QUENCH_AREAS - 1).astype(jnp.int32),
        "region_threshold_kelvin": jnp.clip(jax.random.uniform(arg_keys[8], (QUENCH_AREAS,), jnp.float32, 5.0, 12.0), 5.0, 12.0),
    }


def make_tile(rows_geom, cols_geom):
    dist = (rows_geom[0][:, None] - cols_geom[0][None, :]) ** 2
    dist = dist + (rows_geom[1][:, None] - cols_geom[1][None, :]) ** 2
    dist = dist + (rows_geom[2][:, None] - cols_geom[2][None, :]) ** 2
    soft = rows_geom[6][:, None] ** 2 + cols_geom[6][None, :] ** 2
    inner = rows_geom[3][:, None] * cols_geom[3][None, :]
    inner = inner + rows_geom[4][:, None] * cols_geom[4][None, :]
    inner = inner + rows_geom[5][:, None] * cols_geom[5][None, :]
    return (inner / jnp.sqrt(dist + soft)).astype(jnp.bfloat16)

def block_product(rows_geom, cols_geom, cols_vec):
    count = rows_geom.shape[1]
    width = math.gcd(count, 1024)
    blocks = rows_geom.reshape(7, count // width, width).transpose(1, 0, 2)

    def one_block(geom):
        tile = make_tile(geom, cols_geom)
        return jnp.einsum('kc,rc->kr', cols_vec.astype(jnp.float32), tile.astype(jnp.float32), preferred_element_type=jnp.float32)
    out = lax.map(one_block, blocks)
    return out.transpose(1, 0, 2).reshape(cols_vec.shape[0], count)

def gathered_entries(ids, table):
    levels = jnp.arange(table.shape[0], dtype=jnp.int32)
    match = ids[None, :] == levels[:, None]
    return lax.optimization_barrier(jnp.sum(jnp.where(match, table[:, None], jnp.float32(0.0)), axis=0))

def reference(strand_layout, strand_amperes_panel, krylov_vectors, strand_kelvin, strand_ohmic_value, strand_warmer_slot, warmer_kelvin_gain, strand_region_slot, region_threshold_kelvin):
    hi = lax.Precision.HIGHEST
    q_wire = strand_amperes_panel.astype(jnp.bfloat16)
    flux = block_product(strand_layout, strand_layout, q_wire)
    warmer_increment = gathered_entries(strand_warmer_slot, warmer_kelvin_gain)
    threshold_kelvin = gathered_entries(strand_region_slot, region_threshold_kelvin)
    ohmic_specific_value = strand_ohmic_value * jax.nn.sigmoid(strand_kelvin + warmer_increment - threshold_kelvin)
    joule = ohmic_specific_value * lax.optimization_barrier(jnp.mean(strand_amperes_panel * strand_amperes_panel, axis=0))
    image = ohmic_specific_value[None, :] * strand_amperes_panel + flux
    hess = jnp.dot(krylov_vectors, image.T, precision=hi)
    resid = image - jnp.dot(hess.T, krylov_vectors, precision=hi)
    gram = jnp.dot(resid, resid.T, precision=hi)
    chol = jnp.linalg.cholesky(gram)
    q_next = jax.scipy.linalg.solve_triangular(chol, resid, lower=True)
    return (q_next, hess, chol, joule)
```

```python
import functools

import jax
import jax.numpy as jnp
from jax import lax
from jax.experimental import pallas as pl
from jax.experimental.pallas import tpu as pltpu
from jax.sharding import PartitionSpec as P

HI = lax.Precision.HIGHEST
F32 = jnp.float32
BF16 = jnp.bfloat16
NT = (((1,), (1,)), ((), ()))
SECTIONS = 16
ROW_GROUP = 1024
ROW_TILE = 256
COL_TILE = 1024
COL_STEP = 2048
BLOCKS = ((1, 0), (1, 1), (3, 0), (3, 1), (2, 0), (2, 1), (0, 1), (0, 0))


def small_call(body, args, shapes, name, scalars=0):
    whole = pl.BlockSpec(memory_space=pltpu.VMEM)
    scalar = pl.BlockSpec(memory_space=pltpu.SMEM)
    return pl.pallas_call(
        body,
        in_specs=[whole] * (len(args) - scalars) + [scalar] * scalars,
        out_specs=[whole] * len(shapes),
        out_shape=[jax.ShapeDtypeStruct(shape, dtype) for shape, dtype in shapes],
        compiler_params=pltpu.CompilerParams(vmem_limit_bytes=16 * 2**20),
        name=name,
    )(*args)


def pieces(value, count):
    out = []
    for _ in range(count):
        piece = value.astype(BF16).astype(F32)
        out.append(piece)
        value = value - piece
    return out


def payload_body(layout_ref, amps_ref, out_ref):
    layout = layout_ref[...]
    high, low = pieces(layout[0:3] - 0.5, 2)
    centre = high + low
    square = centre * centre
    soft = square[0:1] + square[1:2] + square[2:3] + layout[6:7] * layout[6:7]
    parts = [high, low, *pieces(soft, 3), *pieces(layout[3:6], 2), jnp.ones_like(soft)]
    out_ref[0:16, :] = jnp.concatenate(parts, axis=0).astype(BF16)
    out_ref[16:32, :] = amps_ref[...].astype(BF16)


def heat_body(kelvin_ref, ohmic_ref, warmer_ref, region_ref, amps_ref, gain_ref, limit_ref, rho_ref, joule_ref):
    def entries(ids, table_ref):
        out = jnp.zeros(ids.shape, F32)
        for level in range(table_ref.shape[0]):
            out = jnp.where(ids == level, table_ref[level], out)
        return out

    warm = entries(warmer_ref[...], gain_ref)
    limit = entries(region_ref[...], limit_ref)
    rho = ohmic_ref[...] / (1.0 + jnp.exp(limit - (kelvin_ref[...] + warm)))
    amps = amps_ref[...]
    rho_ref[...] = rho
    joule_ref[...] = rho * jnp.mean(amps * amps, axis=0, keepdims=True)


def row_features(rows):
    high, low = rows[0:3], rows[3:6]
    zero = jnp.zeros_like(rows[0:1])
    one = jnp.ones_like(zero)
    first = [-2 * high, -2 * high, one, one, one] + [zero] * 6 + [rows[6:7]]
    second = [-2 * low, -2 * low] + [zero] * 9 + [rows[7:8]]
    third = [zero] * 15 + [rows[8:9]]
    return jnp.concatenate(first + second + third, axis=0).T


def flux_body(has_acc, finish, row0, cols_ref, a_ref, *refs):
    acc_ref = s_ref = krylov_ref = None
    if has_acc:
        acc_ref, refs = refs[0], refs[1:]
    if finish:
        s_ref, krylov_ref, refs = refs[0], refs[1], refs[2:]
    out_ref, b_scr, w_scr = refs[:3]
    total = refs[3] if finish else out_ref
    step, group = pl.program_id(0), pl.program_id(1)
    width = cols_ref.shape[2]
    span = b_scr.shape[1]
    chunks = span // width
    base = pl.multiple_of(group * ROW_GROUP, ROW_GROUP)

    @pl.when(group == 0)
    def _():
        for y in range(chunks):
            at = slice(y * width, (y + 1) * width)
            geo = cols_ref[step * chunks + y, 0:16, :]
            b_scr[0:16, at] = geo
            b_scr[16:32, at] = geo
            b_scr[32:48, at] = geo
            wide = geo.astype(F32)
            wire = cols_ref[step * chunks + y, 16:32, :].astype(F32)
            for c in range(3):
                seg = wide[9 + c : 10 + c] + wide[12 + c : 13 + c]
                w_scr[16 * c : 16 * (c + 1), at] = (wire * seg).astype(BF16)

    @pl.when(step == 0)
    def _():
        here = pl.ds(base, ROW_GROUP)
        if has_acc:
            total[here, :] = acc_ref[pl.ds(pl.multiple_of(row0 + base, ROW_GROUP), ROW_GROUP), :]
        else:
            total[here, :] = jnp.zeros((ROW_GROUP, total.shape[1]), F32)

    for k in range(ROW_GROUP // ROW_TILE):
        here = pl.ds(pl.multiple_of(base + k * ROW_TILE, ROW_TILE), ROW_TILE)
        there = pl.ds(pl.multiple_of(row0 + base + k * ROW_TILE, ROW_TILE), ROW_TILE)
        a = a_ref[there, :]
        sums = None
        for j in range(span // COL_TILE):
            at = slice(j * COL_TILE, (j + 1) * COL_TILE)
            r2 = jnp.dot(a, b_scr[:, at], preferred_element_type=F32)
            tile = lax.rsqrt(r2).astype(BF16)
            part = lax.dot_general(tile, w_scr[:, at], NT, preferred_element_type=F32)
            sums = part if sums is None else sums + part
        total[here, :] += sums

    if finish:

        @pl.when(step == pl.num_programs(0) - 1)
        def _():
            for k in range(ROW_GROUP // width):
                here = pl.ds(pl.multiple_of(base + k * width, width), width)
                turned = total[here, :].T
                block = group * (ROW_GROUP // width) + k
                seg = s_ref[row0 // width + block]
                out_ref[block, 0:16, :] = (
                    turned[0:16] * seg[0:1] + turned[16:32] * seg[1:2] + turned[32:48] * seg[2:3]
                )

        @pl.when((step == 0) & (group == 0))
        def _():
            krylov = krylov_ref[...]
            kk_scr = refs[4]
            kk_scr[...] = lax.dot_general(
                krylov, krylov, NT, precision=HI, preferred_element_type=F32
            )
            me = lax.axis_index("row")
            for n in range(out_ref.shape[0]):
                shift, swap = BLOCKS[row0 // width + n]
                owner = (me // 2 + 4 - shift) % 4 * 2 + (me + swap) % 2
                out_ref[n, 16:24, :] = jnp.zeros((8, width), F32)
                out_ref[n, 16:24, 0:64] = kk_scr[pl.ds(pl.multiple_of(owner * 8, 8), 8), :]


def flux_call(cols, a, acc=None, seg=None, krylov=None, row0=0, rows=None):
    rows = a.shape[0] if rows is None else rows
    chunks, _, width = cols.shape
    finish = seg is not None
    whole = pl.BlockSpec(memory_space=pltpu.VMEM)
    args = [cols, a]
    if acc is not None:
        args.append(acc)
    if finish:
        args += [seg, krylov]
        shape = jax.ShapeDtypeStruct((rows // width, SECTIONS + 8, width), F32)
    else:
        shape = jax.ShapeDtypeStruct((rows, 3 * SECTIONS), F32)
    scratch = [pltpu.VMEM((48, COL_STEP), BF16), pltpu.VMEM((48, COL_STEP), BF16)]
    if finish:
        scratch += [pltpu.VMEM((rows, 3 * SECTIONS), F32), pltpu.VMEM((64, 64), F32)]
    pairs = rows * chunks * width
    return pl.pallas_call(
        functools.partial(flux_body, acc is not None, finish, row0),
        grid=(chunks * width // COL_STEP, rows // ROW_GROUP),
        in_specs=[whole] * len(args),
        out_specs=whole,
        out_shape=shape,
        scratch_shapes=scratch,
        compiler_params=pltpu.CompilerParams(vmem_limit_bytes=40 * 2**20),
        cost_estimate=pl.CostEstimate(
            flops=pairs * 2 * 512, bytes_accessed=4 * rows * 128, transcendentals=pairs
        ),
        name="flux",
    )(*args)


def image_body(sent1, sent3, sent2, mine_ref, swap_ref, rho_ref, amps_ref, krylov_ref, image_ref, stats_ref):
    flux = (sent1[0] + sent3[0] + sent2[0] + mine_ref[1]) + swap_ref[...]
    image = rho_ref[...] * amps_ref[...] + flux[0:16]
    image_ref[...] = image
    kk = flux[16:24, 0:64]
    dot = functools.partial(
        lax.dot_general, dimension_numbers=NT, precision=HI, preferred_element_type=F32
    )
    parts = [
        dot(image, krylov_ref[...]),
        dot(image, image),
        jnp.concatenate([kk[:, 0:32], kk[:, 32:64]], axis=0),
        jnp.zeros((SECTIONS, 16), F32),
    ]
    stats = jnp.concatenate(parts, axis=1)
    for n in range(stats_ref.shape[0]):
        stats_ref[n] = stats


def end_body(krylov_ref, image_ref, stats_ref, q_ref, hess_ref, chol_ref, kk_scr):
    dot = functools.partial(lax.dot_general, precision=HI, preferred_element_type=F32)
    nn = (((1,), (0,)), ((), ()))
    stats = stats_ref[0]
    for n in range(1, stats_ref.shape[0]):
        stats = stats + stats_ref[n]
    for n in range(stats_ref.shape[0]):
        kk_scr[8 * n : 8 * n + 8, 0:32] = stats_ref[n, 0:8, 80:112]
        kk_scr[8 * n : 8 * n + 8, 32:64] = stats_ref[n, 8:16, 80:112]
    turned = stats[:, 0:64]
    hess_ref[...] = turned
    kh = dot(turned, kk_scr[...], nn)
    gram = stats[:, 64:80] + dot(kh - 2.0 * turned, turned, NT)
    resid = image_ref[...] - dot(turned, krylov_ref[...], nn)
    row = lax.broadcasted_iota(jnp.int32, gram.shape, 0)
    col = lax.broadcasted_iota(jnp.int32, gram.shape, 1)
    tall = lax.broadcasted_iota(jnp.int32, resid.shape, 0)
    chol = jnp.zeros_like(gram)
    for j in range(SECTIONS):
        root = jnp.sqrt(gram[j : j + 1, j : j + 1])
        column = gram[:, j : j + 1] / root
        across = gram[j : j + 1, :] / root
        column = jnp.where(row[:, 0:1] >= j, column, 0.0)
        chol = jnp.where(col == j, column, chol)
        solved = resid[j : j + 1, :] / root
        gram = gram - column * across
        resid = jnp.where(tall == j, solved, resid - jnp.where(tall > j, column * solved, 0.0))
    q_ref[...] = resid
    chol_ref[...] = chol


def end_call(krylov, image, stats):
    whole = pl.BlockSpec(memory_space=pltpu.VMEM)
    return pl.pallas_call(
        end_body,
        in_specs=[whole] * 3,
        out_specs=[whole] * 3,
        out_shape=[
            jax.ShapeDtypeStruct(image.shape, F32),
            jax.ShapeDtypeStruct((SECTIONS, krylov.shape[0]), F32),
            jax.ShapeDtypeStruct((SECTIONS, SECTIONS), F32),
        ],
        scratch_shapes=[pltpu.VMEM((64, 64), F32)],
        compiler_params=pltpu.CompilerParams(vmem_limit_bytes=16 * 2**20),
        name="finish",
    )(krylov, image, stats)


def core_swap(value):
    return lax.ppermute(value, "row", [(i, i ^ 1) for i in range(8)])


def shift_x(value, k):
    return lax.ppermute(value, "row", [(i, (i + 2 * k) % 8) for i in range(8)])


def shift_y(value, k):
    return lax.ppermute(value, "col", [(i, (i + 8 * k) % 32) for i in range(32)])


def swap_z(value, k):
    return lax.ppermute(value, "col", [(i, i ^ k) for i in range(32)])


def local(
    strand_layout,
    strand_amperes_panel,
    krylov_vectors,
    strand_kelvin,
    strand_ohmic_value,
    strand_warmer_slot,
    warmer_kelvin_gain,
    strand_region_slot,
    region_threshold_kelvin,
):
    width = strand_kelvin.shape[0]
    own = small_call(
        payload_body, (strand_layout, strand_amperes_panel), [((32, width), BF16)], "payload"
    )[0]
    pair = jnp.stack([own, core_swap(own)])
    others = [shift_x(pair, k) for k in (1, 3, 2)]
    column = jnp.stack([own] + [shift_y(own, k) for k in (1, 3, 2)])

    rows = jnp.concatenate(others + [pair[::-1]], axis=0)
    seg = rows[:, 9:12].astype(F32) + rows[:, 12:15].astype(F32)
    seg = jnp.concatenate([seg, jnp.zeros((8, 5, seg.shape[2]), F32)], axis=1)
    a = row_features(rows.transpose(1, 0, 2).reshape(32, -1))

    far = swap_z(column, 4)
    acc = flux_call(column, a)
    column = jnp.concatenate([column, far], axis=0)
    middle = swap_z(column, 2)
    acc = flux_call(far, a, acc)
    column = jnp.concatenate([column, middle], axis=0)
    near = swap_z(column, 1)
    acc = flux_call(middle, a, acc)
    away = flux_call(near, a, acc, seg, krylov_vectors, 0, 3072)
    sent = [shift_x(away[2 * n : 2 * n + 2], -k) for n, k in enumerate((1, 3, 2))]
    mine = flux_call(near, a, acc, seg, krylov_vectors, 3072, 1024)
    swapped = core_swap(sent[0][1] + sent[1][1] + sent[2][1] + mine[0])

    flat = (strand_kelvin, strand_ohmic_value, strand_warmer_slot, strand_region_slot)
    rho, joule = small_call(
        heat_body,
        (*(v[None] for v in flat), strand_amperes_panel, warmer_kelvin_gain, region_threshold_kelvin),
        [((1, width), F32)] * 2,
        "heat",
        2,
    )
    image, stats = small_call(
        image_body,
        (*sent, mine, swapped, rho, strand_amperes_panel, krylov_vectors),
        [((SECTIONS, width), F32), ((32, SECTIONS, 128), F32)],
        "image",
    )
    stats = jnp.sum(lax.all_to_all(stats, "col", 0, 0), axis=0)
    stats = lax.all_to_all(jnp.broadcast_to(stats[None], (8, *stats.shape)), "row", 0, 0)
    q_next, hess, chol = end_call(krylov_vectors, image, stats)
    return (q_next, hess.T, chol, joule[0])


def solution(mesh):
    return jax.shard_map(
        local,
        mesh=mesh,
        in_specs=(
            P(None, ("row", "col")),
            P(None, ("row", "col")),
            P(None, ("row", "col")),
            P(("row", "col")),
            P(("row", "col")),
            P(("row", "col")),
            P(),
            P(("row", "col")),
            P(),
        ),
        out_specs=(P(None, ("row", "col")), P(), P(), P(("row", "col"))),
        check_vma=False,
    )
```

```python
import functools

import jax
import jax.numpy as jnp
from jax import lax
from jax.experimental import pallas as pl
from jax.experimental.pallas import tpu as pltpu
from jax.sharding import PartitionSpec as P

HI = lax.Precision.HIGHEST
F32 = jnp.float32
BF16 = jnp.bfloat16
NT = (((1,), (1,)), ((), ()))
SECTIONS = 16
ROW_TILE = 256
COL_TILE = 1024
CORE_Z = [
    [(2 * x + c) * 32 + 8 * y + z for c in range(2) for z in range(8)]
    for x in range(4)
    for y in range(4)
]
X_Y = [
    [(2 * x + c) * 32 + 8 * y + z for x in range(4) for y in range(4)]
    for c in range(2)
    for z in range(8)
]
BLOCKS = ((1, 0), (1, 1), (3, 0), (3, 1), (2, 0), (2, 1), (0, 1), (0, 0))


def small_call(body, args, shapes, name, scalars=0):
    whole = pl.BlockSpec(memory_space=pltpu.VMEM)
    scalar = pl.BlockSpec(memory_space=pltpu.SMEM)
    return pl.pallas_call(
        body,
        in_specs=[whole] * (len(args) - scalars) + [scalar] * scalars,
        out_specs=[whole] * len(shapes),
        out_shape=[jax.ShapeDtypeStruct(shape, dtype) for shape, dtype in shapes],
        compiler_params=pltpu.CompilerParams(vmem_limit_bytes=16 * 2**20),
        name=name,
    )(*args)


def pieces(value, count):
    out = []
    for _ in range(count):
        piece = value.astype(BF16).astype(F32)
        out.append(piece)
        value = value - piece
    return out


def payload_body(layout_ref, amps_ref, out_ref):
    layout = layout_ref[...]
    high, low = pieces(layout[0:3] - 0.5, 2)
    centre = high + low
    square = centre * centre
    soft = square[0:1] + square[1:2] + square[2:3] + layout[6:7] * layout[6:7]
    parts = [high, low, *pieces(soft, 3), *pieces(layout[3:6], 2), jnp.ones_like(soft)]
    out_ref[0:16, :] = jnp.concatenate(parts, axis=0).astype(BF16)
    out_ref[16:32, :] = amps_ref[...].astype(BF16)


def heat(kelvin_ref, ohmic_ref, warmer_ref, region_ref, amps_ref, gain_ref, limit_ref, rho_ref, joule_ref):
    def entries(ids, table_ref):
        out = jnp.zeros(ids.shape, F32)
        for level in range(table_ref.shape[0]):
            out = jnp.where(ids == level, table_ref[level], out)
        return out

    warm = entries(warmer_ref[...], gain_ref)
    limit = entries(region_ref[...], limit_ref)
    rho = ohmic_ref[...] / (1.0 + jnp.exp(limit - (kelvin_ref[...] + warm)))
    amps = amps_ref[...]
    rho_ref[...] = rho
    joule_ref[...] = rho * jnp.mean(amps * amps, axis=0, keepdims=True)


def row_features(rows):
    high, low = rows[0:3], rows[3:6]
    zero = jnp.zeros_like(rows[0:1])
    one = jnp.ones_like(zero)
    first = [-2 * high, -2 * high, one, one, one] + [zero] * 6 + [rows[6:7]]
    second = [-2 * low, -2 * low] + [zero] * 9 + [rows[7:8]]
    third = [zero] * 15 + [rows[8:9]]
    return jnp.concatenate(first + second + third, axis=0).T


def flux_body(kind, row0, group_rows, cols_ref, a_ref, *refs):
    finish = kind in ("away", "mine")
    acc_ref = s_ref = krylov_ref = None
    heat_in = heat_out = ()
    if kind != "first":
        acc_ref, refs = refs[0], refs[1:]
    if finish:
        s_ref, krylov_ref, refs = refs[0], refs[1], refs[2:]
    if kind == "mine":
        heat_in, refs = refs[:7], refs[7:]
    out_ref, refs = refs[0], refs[1:]
    if kind == "mine":
        heat_out, refs = refs[:2], refs[2:]
    b_scr, w_scr = refs[:2]
    total = refs[2] if finish else out_ref
    step, group = pl.program_id(0), pl.program_id(1)
    width = cols_ref.shape[2]
    span = b_scr.shape[1]
    chunks = span // width
    base = pl.multiple_of(group * group_rows, group_rows)

    @pl.when(group == 0)
    def _():
        for y in range(chunks):
            at = slice(y * width, (y + 1) * width)
            geo = cols_ref[step * chunks + y, 0:16, :]
            b_scr[0:16, at] = geo
            b_scr[16:32, at] = geo
            b_scr[32:48, at] = geo
            wide = geo.astype(F32)
            wire = cols_ref[step * chunks + y, 16:32, :].astype(F32)
            for c in range(3):
                seg = wide[9 + c : 10 + c] + wide[12 + c : 13 + c]
                w_scr[16 * c : 16 * (c + 1), at] = (wire * seg).astype(BF16)

    @pl.when(step == 0)
    def _():
        here = pl.ds(base, group_rows)
        if acc_ref is None:
            total[here, :] = jnp.zeros((group_rows, total.shape[1]), F32)
        else:
            total[here, :] = acc_ref[pl.ds(pl.multiple_of(row0 + base, ROW_TILE), group_rows), :]

    def rows_at(k, offset):
        return pl.ds(pl.multiple_of(offset + base + k * ROW_TILE, ROW_TILE), ROW_TILE)

    def product(tile, at):
        return lax.dot_general(tile, w_scr[:, at], NT, preferred_element_type=F32)

    tiles = [
        (k, slice(j, j + COL_TILE))
        for k in range(group_rows // ROW_TILE)
        for j in range(0, span, COL_TILE)
    ]
    held = None
    for k, at in tiles:
        r2 = jnp.dot(a_ref[rows_at(k, row0), :], b_scr[:, at], preferred_element_type=F32)
        tile = lax.rsqrt(r2).astype(BF16)
        if held is not None:
            total[rows_at(held[0], 0), :] += product(*held[1:])
        held = (k, tile, at)
    total[rows_at(held[0], 0), :] += product(*held[1:])

    if finish:

        @pl.when(step == pl.num_programs(0) - 1)
        def _():
            for k in range(group_rows // width):
                here = pl.ds(pl.multiple_of(base + k * width, width), width)
                turned = total[here, :].T
                block = group * (group_rows // width) + k
                seg = s_ref[row0 // width + block]
                out_ref[block, 0:16, :] = (
                    turned[0:16] * seg[0:1] + turned[16:32] * seg[1:2] + turned[32:48] * seg[2:3]
                )

        @pl.when((step == 0) & (group == 0))
        def _():
            krylov = krylov_ref[...]
            kk_scr = refs[3]
            kk_scr[...] = lax.dot_general(
                krylov, krylov, NT, precision=HI, preferred_element_type=F32
            )
            me = lax.axis_index("row")
            for n in range(out_ref.shape[0]):
                shift, swap = BLOCKS[row0 // width + n]
                owner = (me // 2 + 4 - shift) % 4 * 2 + (me + swap) % 2
                out_ref[n, 16:24, :] = jnp.zeros((8, width), F32)
                out_ref[n, 16:24, 0:64] = kk_scr[pl.ds(pl.multiple_of(owner * 8, 8), 8), :]
            if heat_in:
                heat(*heat_in, *heat_out)


def flux_call(kind, cols, a, *more, row0=0, rows, group_rows, step_chunks):
    chunks, _, width = cols.shape
    finish = kind in ("away", "mine")
    whole = pl.BlockSpec(memory_space=pltpu.VMEM)
    scalar = pl.BlockSpec(memory_space=pltpu.SMEM)
    args = [cols, a, *more]
    specs = [whole] * len(args)
    if finish:
        shapes = [jax.ShapeDtypeStruct((rows // width, SECTIONS + 8, width), F32)]
    else:
        shapes = [jax.ShapeDtypeStruct((rows, 3 * SECTIONS), F32)]
    if kind == "mine":
        specs[-2:] = [scalar] * 2
        shapes += [jax.ShapeDtypeStruct((1, width), F32)] * 2
    span = step_chunks * width
    scratch = [pltpu.VMEM((48, span), BF16), pltpu.VMEM((48, span), BF16)]
    if finish:
        scratch += [pltpu.VMEM((rows, 3 * SECTIONS), F32), pltpu.VMEM((64, 64), F32)]
    pairs = rows * chunks * width
    out = pl.pallas_call(
        functools.partial(flux_body, kind, row0, group_rows),
        grid=(chunks // step_chunks, rows // group_rows),
        in_specs=specs,
        out_specs=[whole] * len(shapes),
        out_shape=shapes,
        scratch_shapes=scratch,
        compiler_params=pltpu.CompilerParams(vmem_limit_bytes=40 * 2**20),
        cost_estimate=pl.CostEstimate(
            flops=pairs * 2 * 512, bytes_accessed=4 * rows * 128, transcendentals=pairs
        ),
        name="flux",
    )(*args)
    return out if kind == "mine" else out[0]


def image_body(sent1, sent3, sent2, mine_ref, swap_ref, rho_ref, amps_ref, krylov_ref, image_ref, stats_ref):
    flux = (sent1[0] + sent3[0] + sent2[0] + mine_ref[1]) + swap_ref[...]
    image = rho_ref[...] * amps_ref[...] + flux[0:16]
    image_ref[...] = image
    kk = flux[16:24, 0:64]
    dot = functools.partial(
        lax.dot_general, dimension_numbers=NT, precision=HI, preferred_element_type=F32
    )
    parts = [
        dot(image, krylov_ref[...]),
        dot(image, image),
        jnp.concatenate([kk[:, 0:32], kk[:, 32:64]], axis=0),
        jnp.zeros((SECTIONS, 16), F32),
    ]
    stats = jnp.concatenate(parts, axis=1)
    for n in range(stats_ref.shape[0]):
        stats_ref[n] = stats


def middle_body(in_ref, out_ref):
    halves = []
    for c in range(2):
        half = in_ref[8 * c]
        for z in range(1, 8):
            half = half + in_ref[8 * c + z]
        halves.append(half)
    lane = lax.broadcasted_iota(jnp.int32, halves[0].shape, 1)
    main = jnp.where(lane < 80, halves[0] + halves[1], halves[0])
    other = halves[1]
    parts = [other[0:8, 80:112], other[8:16, 80:112], jnp.zeros((8, 64), F32)]
    extra = jnp.concatenate(parts, axis=1)
    for n in range(16):
        out_ref[n, 0:16, :] = main
        out_ref[n, 16:24, :] = extra


def end_body(krylov_ref, image_ref, stats_ref, q_ref, hess_ref, chol_ref, kk_scr):
    dot = functools.partial(lax.dot_general, precision=HI, preferred_element_type=F32)
    nn = (((1,), (0,)), ((), ()))
    stats = None
    for x in range(4):
        part = stats_ref[4 * x]
        for y in range(1, 4):
            part = part + stats_ref[4 * x + y]
        kk_scr[16 * x : 16 * x + 8, 0:32] = part[0:8, 80:112]
        kk_scr[16 * x : 16 * x + 8, 32:64] = part[8:16, 80:112]
        kk_scr[16 * x + 8 : 16 * x + 16, :] = part[16:24, 0:64]
        stats = part if stats is None else stats + part
    stats = stats[0:16]
    turned = stats[:, 0:64]
    hess_ref[...] = turned
    kh = dot(turned, kk_scr[...], nn)
    gram = stats[:, 64:80] + dot(kh - 2.0 * turned, turned, NT)
    resid = image_ref[...] - dot(turned, krylov_ref[...], nn)
    row = lax.broadcasted_iota(jnp.int32, gram.shape, 0)
    col = lax.broadcasted_iota(jnp.int32, gram.shape, 1)
    tall = lax.broadcasted_iota(jnp.int32, resid.shape, 0)
    chol = jnp.zeros_like(gram)
    for j in range(SECTIONS):
        scale = 1.0 / jnp.sqrt(gram[j : j + 1, j : j + 1])
        column = jnp.where(row[:, 0:1] >= j, gram[:, j : j + 1] * scale, 0.0)
        across = gram[j : j + 1, :] * scale
        chol = jnp.where(col == j, column, chol)
        solved = resid[j : j + 1, :] * scale
        gram = gram - column * across
        resid = jnp.where(tall == j, solved, resid - jnp.where(tall > j, column * solved, 0.0))
    q_ref[...] = resid
    chol_ref[...] = chol


def end_call(krylov, image, stats):
    whole = pl.BlockSpec(memory_space=pltpu.VMEM)
    return pl.pallas_call(
        end_body,
        in_specs=[whole] * 3,
        out_specs=[whole] * 3,
        out_shape=[
            jax.ShapeDtypeStruct(image.shape, F32),
            jax.ShapeDtypeStruct((SECTIONS, krylov.shape[0]), F32),
            jax.ShapeDtypeStruct((SECTIONS, SECTIONS), F32),
        ],
        scratch_shapes=[pltpu.VMEM((64, 64), F32)],
        compiler_params=pltpu.CompilerParams(vmem_limit_bytes=16 * 2**20),
        name="finish",
    )(krylov, image, stats)


def core_swap(value):
    return lax.ppermute(value, "row", [(i, i ^ 1) for i in range(8)])


def shift_x(value, k):
    return lax.ppermute(value, "row", [(i, (i + 2 * k) % 8) for i in range(8)])


def shift_y(value, k):
    return lax.ppermute(value, "col", [(i, (i + 8 * k) % 32) for i in range(32)])


def swap_z(value, k):
    return lax.ppermute(value, "col", [(i, i ^ k) for i in range(32)])


def local(
    strand_layout,
    strand_amperes_panel,
    krylov_vectors,
    strand_kelvin,
    strand_ohmic_value,
    strand_warmer_slot,
    warmer_kelvin_gain,
    strand_region_slot,
    region_threshold_kelvin,
):
    width = strand_kelvin.shape[0]
    own = small_call(
        payload_body, (strand_layout, strand_amperes_panel), [((32, width), BF16)], "payload"
    )[0]
    pair = jnp.stack([own, core_swap(own)])
    others = [shift_x(pair, k) for k in (1, 3, 2)]
    column = jnp.stack([own] + [shift_y(own, k) for k in (1, 3, 2)])

    rows = jnp.concatenate(others + [pair[::-1]], axis=0)
    seg = rows[:, 9:12].astype(F32) + rows[:, 12:15].astype(F32)
    seg = jnp.concatenate([seg, jnp.zeros((8, 5, seg.shape[2]), F32)], axis=1)
    a = row_features(rows.transpose(1, 0, 2).reshape(32, -1))

    count = a.shape[0]
    far = swap_z(column, 4)
    acc = flux_call("first", column[:2], a, rows=count, group_rows=2048, step_chunks=2)
    whole = jnp.concatenate([column, far], axis=0)
    middle = swap_z(whole, 2)
    acc = flux_call("next", whole[2:], a, acc, rows=count, group_rows=1024, step_chunks=6)
    whole = jnp.concatenate([whole, middle], axis=0)
    near = swap_z(whole, 1)
    acc = flux_call("next", middle, a, acc, rows=count, group_rows=1024, step_chunks=8)
    away = flux_call(
        "away", near, a, acc, seg, krylov_vectors, rows=3072, group_rows=1024, step_chunks=8
    )
    sent = [shift_x(away[2 * n : 2 * n + 2], -k) for n, k in enumerate((1, 3, 2))]
    flat = (strand_kelvin, strand_ohmic_value, strand_warmer_slot, strand_region_slot)
    mine, rho, joule = flux_call(
        "mine", near, a, acc, seg, krylov_vectors, *(v[None] for v in flat), strand_amperes_panel,
        warmer_kelvin_gain, region_threshold_kelvin,
        row0=3072, rows=1024, group_rows=1024, step_chunks=8,
    )
    swapped = core_swap(sent[0][1] + sent[1][1] + sent[2][1] + mine[0])

    image, stats = small_call(
        image_body,
        (*sent, mine, swapped, rho, strand_amperes_panel, krylov_vectors),
        [((SECTIONS, width), F32), ((16, SECTIONS, 128), F32)],
        "image",
    )
    stats = lax.all_to_all(stats, ("row", "col"), 0, 0, axis_index_groups=CORE_Z)
    stats = small_call(middle_body, (stats,), [((16, 24, 128), F32)], "middle")[0]
    stats = lax.all_to_all(stats, ("row", "col"), 0, 0, axis_index_groups=X_Y)
    q_next, hess, chol = end_call(krylov_vectors, image, stats)
    return (q_next, hess.T, chol, joule[0])


def solution(mesh):
    return jax.shard_map(
        local,
        mesh=mesh,
        in_specs=(
            P(None, ("row", "col")),
            P(None, ("row", "col")),
            P(None, ("row", "col")),
            P(("row", "col")),
            P(("row", "col")),
            P(("row", "col")),
            P(),
            P(("row", "col")),
            P(),
        ),
        out_specs=(P(None, ("row", "col")), P(), P(), P(("row", "col"))),
        check_vma=False,
    )
```

```python
import functools

import jax
import jax.numpy as jnp
from jax import lax
from jax.experimental import pallas as pl
from jax.experimental.pallas import tpu as pltpu
from jax.sharding import PartitionSpec as P

HI = lax.Precision.HIGHEST
F32 = jnp.float32
BF16 = jnp.bfloat16
NT = (((1,), (1,)), ((), ()))
SECTIONS = 16
ROW_TILE = 1024
COL_TILE = 256
CORE_Z = [
    [(2 * x + c) * 32 + 8 * y + z for c in range(2) for z in range(8)]
    for x in range(4)
    for y in range(4)
]
X_Y = [
    [(2 * x + c) * 32 + 8 * y + z for x in range(4) for y in range(4)]
    for c in range(2)
    for z in range(8)
]
BLOCKS = ((1, 0), (1, 1), (3, 0), (3, 1), (2, 0), (2, 1), (0, 1), (0, 0))


def small_call(body, args, shapes, name, limit=16):
    whole = pl.BlockSpec(memory_space=pltpu.VMEM)
    return pl.pallas_call(
        body,
        in_specs=[whole] * len(args),
        out_specs=[whole] * len(shapes),
        out_shape=[jax.ShapeDtypeStruct(shape, dtype) for shape, dtype in shapes],
        compiler_params=pltpu.CompilerParams(vmem_limit_bytes=limit * 2**20),
        name=name,
    )(*args)


def pieces(value, count):
    out = []
    for _ in range(count):
        piece = value.astype(BF16).astype(F32)
        out.append(piece)
        value = value - piece
    return out


def payload_body(layout_ref, amps_ref, out_ref):
    layout = layout_ref[...]
    high, low = pieces(layout[0:3] - 0.5, 2)
    centre = high + low
    square = centre * centre
    soft = square[0:1] + square[1:2] + square[2:3] + layout[6:7] * layout[6:7]
    parts = [high, low, *pieces(soft, 3), *pieces(layout[3:6], 2), jnp.ones_like(soft)]
    out_ref[0:16, :] = jnp.concatenate(parts, axis=0).astype(BF16)
    out_ref[16:32, :] = amps_ref[...].astype(BF16)


def heat(kelvin_ref, ohmic_ref, warmer_ref, region_ref, amps_ref, gain_ref, limit_ref, rho_ref, joule_ref):
    def entries(ids, table_ref):
        out = jnp.zeros(ids.shape, F32)
        for level in range(table_ref.shape[0]):
            out = jnp.where(ids == level, table_ref[level], out)
        return out

    warm = entries(warmer_ref[...], gain_ref)
    limit = entries(region_ref[...], limit_ref)
    rho = ohmic_ref[...] / (1.0 + jnp.exp(limit - (kelvin_ref[...] + warm)))
    amps = amps_ref[...]
    rho_ref[...] = rho
    joule_ref[...] = rho * jnp.mean(amps * amps, axis=0, keepdims=True)


def row_features(rows):
    high, low = rows[0:3], rows[3:6]
    zero = jnp.zeros_like(rows[0:1])
    one = jnp.ones_like(zero)
    first = [-2 * high, -2 * high, one, one, one] + [zero] * 6 + [rows[6:7]]
    second = [-2 * low, -2 * low] + [zero] * 9 + [rows[7:8]]
    third = [zero] * 15 + [rows[8:9]]
    return jnp.concatenate(first + second + third, axis=0)


def flux_body(kind, row0, group_rows, cols_ref, a_ref, *refs):
    finish = kind in ("away", "mine")
    acc_ref = None
    if kind != "first":
        acc_ref, refs = refs[0], refs[1:]
    if finish:
        s_ref, refs = refs[0], refs[1:]
    if kind == "away":
        krylov_ref, heat_in, refs = refs[0], refs[1:8], refs[8:]
    if kind == "mine":
        kk_ref, refs = refs[0], refs[1:]
    out_ref, refs = refs[0], refs[1:]
    if kind == "away":
        kk_ref, heat_out, refs = refs[0], refs[1:3], refs[3:]
    b_scr, w_scr = refs[:2]
    total = refs[2] if finish else out_ref
    step, group = pl.program_id(0), pl.program_id(1)
    width = cols_ref.shape[2]
    span = w_scr.shape[1]
    chunks = span // width
    base = pl.multiple_of(group * group_rows, group_rows)

    @pl.when(group == 0)
    def _():
        for y in range(chunks):
            at = slice(y * width, (y + 1) * width)
            geo = cols_ref[step * chunks + y, 0:16, :].astype(F32)
            wire = cols_ref[step * chunks + y, 16:32, :].astype(F32)
            b_scr[at, :] = jnp.concatenate([geo, geo, geo], axis=0).T.astype(BF16)
            for c in range(3):
                seg = geo[9 + c : 10 + c] + geo[12 + c : 13 + c]
                w_scr[16 * c : 16 * (c + 1), at] = (wire * seg).astype(BF16)

    def rows_at(k, offset):
        return pl.ds(pl.multiple_of(offset + base + k * ROW_TILE, ROW_TILE), ROW_TILE)

    @pl.when(step == 0)
    def _():
        for k in range(group_rows // ROW_TILE):
            if acc_ref is None:
                total[:, rows_at(k, 0)] = jnp.zeros((3 * SECTIONS, ROW_TILE), F32)
            else:
                total[:, rows_at(k, 0)] = acc_ref[:, rows_at(k, row0)]

    sums = {}

    def add(k, at, tile):
        part = jnp.dot(w_scr[:, at], tile, preferred_element_type=F32)
        sums[k] = sums[k] + part if k in sums else part
        if at.stop == span:
            total[:, rows_at(k, 0)] += sums[k]

    held = None
    for k in range(group_rows // ROW_TILE):
        for j in range(0, span, COL_TILE):
            at = slice(j, j + COL_TILE)
            r2 = jnp.dot(b_scr[at, :], a_ref[:, rows_at(k, row0)], preferred_element_type=F32)
            tile = lax.rsqrt(r2).astype(BF16)
            if held is not None:
                add(*held)
            held = (k, at, tile)
    add(*held)

    if finish:

        @pl.when(step == pl.num_programs(0) - 1)
        def _():
            for k in range(group_rows // width):
                here = pl.ds(pl.multiple_of(base + k * width, width), width)
                turned = total[:, here]
                block = group * (group_rows // width) + k
                seg = s_ref[row0 // width + block]
                out_ref[block, 0:16, :] = (
                    turned[0:16] * seg[0:1] + turned[16:32] * seg[1:2] + turned[32:48] * seg[2:3]
                )

        @pl.when((step == 0) & (group == 0))
        def _():
            if kind == "away":
                krylov = krylov_ref[...]
                kk_ref[...] = lax.dot_general(
                    krylov, krylov, NT, precision=HI, preferred_element_type=F32
                )
                heat(*heat_in, *heat_out)
            me = lax.axis_index("row")
            for n in range(out_ref.shape[0]):
                shift, swap = BLOCKS[row0 // width + n]
                owner = (me // 2 + 4 - shift) % 4 * 2 + (me + swap) % 2
                out_ref[n, 16:24, :] = jnp.zeros((8, width), F32)
                out_ref[n, 16:24, 0:64] = kk_ref[pl.ds(pl.multiple_of(owner * 8, 8), 8), :]


def flux_call(kind, cols, a, *more, row0=0, rows, group_rows, step_chunks):
    chunks, _, width = cols.shape
    finish = kind in ("away", "mine")
    whole = pl.BlockSpec(memory_space=pltpu.VMEM)
    scalar = pl.BlockSpec(memory_space=pltpu.SMEM)
    args = [cols, a, *more]
    specs = [whole] * len(args)
    if finish:
        shapes = [jax.ShapeDtypeStruct((rows // width, SECTIONS + 8, width), F32)]
    else:
        shapes = [jax.ShapeDtypeStruct((3 * SECTIONS, rows), F32)]
    if kind == "away":
        specs[-2:] = [scalar] * 2
        shapes += [jax.ShapeDtypeStruct((64, 64), F32)]
        shapes += [jax.ShapeDtypeStruct((1, width), F32)] * 2
    span = step_chunks * width
    scratch = [pltpu.VMEM((span, 48), BF16), pltpu.VMEM((48, span), BF16)]
    if finish:
        scratch.append(pltpu.VMEM((3 * SECTIONS, rows), F32))
    pairs = rows * chunks * width
    out = pl.pallas_call(
        functools.partial(flux_body, kind, row0, group_rows),
        grid=(chunks // step_chunks, rows // group_rows),
        in_specs=specs,
        out_specs=[whole] * len(shapes),
        out_shape=shapes,
        scratch_shapes=scratch,
        compiler_params=pltpu.CompilerParams(vmem_limit_bytes=40 * 2**20),
        cost_estimate=pl.CostEstimate(
            flops=pairs * 2 * 512, bytes_accessed=4 * rows * 128, transcendentals=pairs
        ),
        name="flux",
    )(*args)
    return out if kind == "away" else out[0]


def image_body(sent1, sent3, sent2, mine_ref, swap_ref, rho_ref, amps_ref, krylov_ref, image_ref, stats_ref):
    flux = (sent1[0] + sent3[0] + sent2[0] + mine_ref[1]) + swap_ref[...]
    image = rho_ref[...] * amps_ref[...] + flux[0:16]
    image_ref[...] = image
    kk = flux[16:24, 0:64]
    dot = functools.partial(
        lax.dot_general, dimension_numbers=NT, precision=HI, preferred_element_type=F32
    )
    parts = [
        dot(image, krylov_ref[...]),
        dot(image, image),
        jnp.concatenate([kk[:, 0:32], kk[:, 32:64]], axis=0),
        jnp.zeros((SECTIONS, 16), F32),
    ]
    stats = jnp.concatenate(parts, axis=1)
    for n in range(stats_ref.shape[0]):
        stats_ref[n] = stats


def middle_body(in_ref, out_ref):
    halves = []
    for c in range(2):
        half = in_ref[8 * c]
        for z in range(1, 8):
            half = half + in_ref[8 * c + z]
        halves.append(half)
    lane = lax.broadcasted_iota(jnp.int32, halves[0].shape, 1)
    main = jnp.where(lane < 80, halves[0] + halves[1], halves[0])
    other = halves[1]
    parts = [other[0:8, 80:112], other[8:16, 80:112], jnp.zeros((8, 64), F32)]
    extra = jnp.concatenate(parts, axis=1)
    for n in range(16):
        out_ref[n, 0:16, :] = main
        out_ref[n, 16:24, :] = extra


def end_body(krylov_ref, image_ref, stats_ref, q_ref, hess_ref, chol_ref, kk_scr):
    dot = functools.partial(lax.dot_general, precision=HI, preferred_element_type=F32)
    nn = (((1,), (0,)), ((), ()))
    stats = None
    for x in range(4):
        part = stats_ref[4 * x]
        for y in range(1, 4):
            part = part + stats_ref[4 * x + y]
        kk_scr[16 * x : 16 * x + 8, 0:32] = part[0:8, 80:112]
        kk_scr[16 * x : 16 * x + 8, 32:64] = part[8:16, 80:112]
        kk_scr[16 * x + 8 : 16 * x + 16, :] = part[16:24, 0:64]
        stats = part if stats is None else stats + part
    stats = stats[0:16]
    turned = stats[:, 0:64]
    hess_ref[...] = turned
    kh = dot(turned, kk_scr[...], nn)
    gram = stats[:, 64:80] + dot(kh - 2.0 * turned, turned, NT)
    resid = image_ref[...] - dot(turned, krylov_ref[...], nn)
    row = lax.broadcasted_iota(jnp.int32, gram.shape, 0)
    col = lax.broadcasted_iota(jnp.int32, gram.shape, 1)
    chol = jnp.zeros_like(gram)
    for j in range(SECTIONS):
        column = gram[:, j : j + 1]
        chol = jnp.where(col == j, column, chol)
        ratio = column / gram[j : j + 1, j : j + 1]
        resid = resid - jnp.where(row[:, 0:1] > j, ratio, 0.0) * resid[j : j + 1, :]
        gram = gram - ratio * gram[j : j + 1, :]
    chol = jnp.where(row >= col, chol, 0.0)
    pivot = jnp.where(row == col, chol, 0.0)
    q_ref[...] = resid / jnp.sqrt(jnp.sum(pivot, axis=1, keepdims=True))
    chol_ref[...] = chol / jnp.sqrt(jnp.sum(pivot, axis=0, keepdims=True))


def end_call(krylov, image, stats):
    whole = pl.BlockSpec(memory_space=pltpu.VMEM)
    return pl.pallas_call(
        end_body,
        in_specs=[whole] * 3,
        out_specs=[whole] * 3,
        out_shape=[
            jax.ShapeDtypeStruct(image.shape, F32),
            jax.ShapeDtypeStruct((SECTIONS, krylov.shape[0]), F32),
            jax.ShapeDtypeStruct((SECTIONS, SECTIONS), F32),
        ],
        scratch_shapes=[pltpu.VMEM((64, 64), F32)],
        compiler_params=pltpu.CompilerParams(vmem_limit_bytes=16 * 2**20),
        name="finish",
    )(krylov, image, stats)


def core_swap(value):
    return lax.ppermute(value, "row", [(i, i ^ 1) for i in range(8)])


def shift_x(value, k):
    return lax.ppermute(value, "row", [(i, (i + 2 * k) % 8) for i in range(8)])


def shift_y(value, k):
    return lax.ppermute(value, "col", [(i, (i + 8 * k) % 32) for i in range(32)])


def swap_z(value, k):
    return lax.ppermute(value, "col", [(i, i ^ k) for i in range(32)])


def local(
    strand_layout,
    strand_amperes_panel,
    krylov_vectors,
    strand_kelvin,
    strand_ohmic_value,
    strand_warmer_slot,
    warmer_kelvin_gain,
    strand_region_slot,
    region_threshold_kelvin,
):
    width = strand_kelvin.shape[0]
    own = small_call(
        payload_body, (strand_layout, strand_amperes_panel), [((32, width), BF16)], "payload"
    )[0]
    ys = [shift_y(own, k) for k in (1, 3)]
    pair = jnp.stack([own, core_swap(own)])
    late, pair = lax.optimization_barrier((own, pair))
    others = [shift_x(pair, k) for k in (1, 3, 2)]
    column = jnp.stack([late] + ys + [shift_y(late, 2)])

    rows = jnp.concatenate(others + [pair[::-1]], axis=0)
    seg = rows[:, 9:12].astype(F32) + rows[:, 12:15].astype(F32)
    seg = jnp.concatenate([seg, jnp.zeros((8, 5, seg.shape[2]), F32)], axis=1)
    a = row_features(rows.transpose(1, 0, 2).reshape(32, -1))
    count = a.shape[1]
    far = swap_z(column, 4)
    acc = flux_call("first", column[:2], a, rows=count, group_rows=2048, step_chunks=2)
    whole = jnp.concatenate([column, far], axis=0)
    middle = swap_z(whole, 2)
    acc = flux_call("next", whole[2:], a, acc, rows=count, group_rows=1024, step_chunks=6)
    whole = jnp.concatenate([whole, middle], axis=0)
    near = swap_z(whole, 1)
    acc = flux_call("next", middle, a, acc, rows=count, group_rows=1024, step_chunks=8)
    flat = (strand_kelvin, strand_ohmic_value, strand_warmer_slot, strand_region_slot)
    away, kk, rho, joule = flux_call(
        "away", near, a, acc, seg, krylov_vectors, *(v[None] for v in flat), strand_amperes_panel,
        warmer_kelvin_gain, region_threshold_kelvin,
        rows=3072, group_rows=1024, step_chunks=8,
    )
    sent = [shift_x(away[2 * n : 2 * n + 2], -k) for n, k in enumerate((1, 3, 2))]
    mine = flux_call(
        "mine", near, a, acc, seg, kk, row0=3072, rows=1024, group_rows=1024, step_chunks=8
    )
    swapped = core_swap(sent[0][1] + sent[1][1] + sent[2][1] + mine[0])

    image, stats = small_call(
        image_body,
        (*sent, mine, swapped, rho, strand_amperes_panel, krylov_vectors),
        [((SECTIONS, width), F32), ((16, SECTIONS, 128), F32)],
        "image",
    )
    stats = lax.all_to_all(stats, ("row", "col"), 0, 0, axis_index_groups=CORE_Z)
    stats = small_call(middle_body, (stats,), [((16, 24, 128), F32)], "middle")[0]
    stats = lax.all_to_all(stats, ("row", "col"), 0, 0, axis_index_groups=X_Y)
    q_next, hess, chol = end_call(krylov_vectors, image, stats)
    return (q_next, hess.T, chol, joule[0])


def solution(mesh):
    return jax.shard_map(
        local,
        mesh=mesh,
        in_specs=(
            P(None, ("row", "col")),
            P(None, ("row", "col")),
            P(None, ("row", "col")),
            P(("row", "col")),
            P(("row", "col")),
            P(("row", "col")),
            P(),
            P(("row", "col")),
            P(),
        ),
        out_specs=(P(None, ("row", "col")), P(), P(), P(("row", "col"))),
        check_vma=False,
    )
```

```python
import functools

import jax
import jax.numpy as jnp
from jax import lax
from jax.experimental import pallas as pl
from jax.experimental.pallas import tpu as pltpu
from jax.sharding import PartitionSpec as P

HI = lax.Precision.HIGHEST
F32 = jnp.float32
BF16 = jnp.bfloat16
NT = (((1,), (1,)), ((), ()))
SECTIONS = 16
ROW_TILE = 1024
COL_TILE = 256
CORE_Z = [
    [(2 * x + c) * 32 + 8 * y + z for c in range(2) for z in range(8)]
    for x in range(4)
    for y in range(4)
]
X_Y = [
    [(2 * x + c) * 32 + 8 * y + z for x in range(4) for y in range(4)]
    for c in range(2)
    for z in range(8)
]
BLOCKS = ((1, 0), (1, 1), (3, 0), (3, 1), (2, 0), (2, 1), (0, 1), (0, 0))


def small_call(body, args, shapes, name, limit=16):
    whole = pl.BlockSpec(memory_space=pltpu.VMEM)
    return pl.pallas_call(
        body,
        in_specs=[whole] * len(args),
        out_specs=[whole] * len(shapes),
        out_shape=[jax.ShapeDtypeStruct(shape, dtype) for shape, dtype in shapes],
        compiler_params=pltpu.CompilerParams(vmem_limit_bytes=limit * 2**20),
        name=name,
    )(*args)


def pieces(value, count):
    out = []
    for _ in range(count):
        piece = value.astype(BF16).astype(F32)
        out.append(piece)
        value = value - piece
    return out


def payload_body(layout_ref, amps_ref, out_ref):
    layout = layout_ref[...]
    high, low = pieces(layout[0:3] - 0.5, 2)
    centre = high + low
    square = centre * centre
    soft = square[0:1] + square[1:2] + square[2:3] + layout[6:7] * layout[6:7]
    parts = [high, low, *pieces(soft, 3), *pieces(layout[3:6], 2), jnp.ones_like(soft)]
    out_ref[0:16, :] = jnp.concatenate(parts, axis=0).astype(BF16)
    out_ref[16:32, :] = amps_ref[...].astype(BF16)


def heat(kelvin_ref, ohmic_ref, warmer_ref, region_ref, amps_ref, gain_ref, limit_ref, rho_ref, joule_ref):
    def entries(ids, table_ref):
        out = jnp.zeros(ids.shape, F32)
        for level in range(table_ref.shape[0]):
            out = jnp.where(ids == level, table_ref[level], out)
        return out

    warm = entries(warmer_ref[...], gain_ref)
    limit = entries(region_ref[...], limit_ref)
    rho = ohmic_ref[...] / (1.0 + jnp.exp(limit - (kelvin_ref[...] + warm)))
    amps = amps_ref[...]
    rho_ref[...] = rho
    joule_ref[...] = rho * jnp.mean(amps * amps, axis=0, keepdims=True)


def rows_body(x1_ref, x3_ref, x2_ref, pair_ref, a_ref, s_ref):
    blocks = [ref[n] for ref in (x1_ref, x3_ref, x2_ref) for n in range(2)]
    blocks += [pair_ref[1], pair_ref[0]]
    width = s_ref.shape[2]
    for n, block in enumerate(blocks):
        geo = block[0:16].astype(F32)
        high, low = -2.0 * geo[0:3], -2.0 * geo[3:6]
        zero = jnp.zeros((15, width), F32)
        one = jnp.ones((3, width), F32)
        parts = [high, high, one, zero[0:6], geo[6:7]]
        parts += [low, low, zero[0:9], geo[7:8], zero, geo[8:9]]
        a_ref[:, n * width : (n + 1) * width] = jnp.concatenate(parts, axis=0).astype(BF16)
        s_ref[n] = jnp.concatenate([geo[9:12] + geo[12:15], zero[0:5]], axis=0)


def flux_body(kind, row0, group_rows, cols_ref, a_ref, *refs):
    finish = kind in ("away", "mine")
    acc_ref = None
    if kind != "first":
        acc_ref, refs = refs[0], refs[1:]
    if finish:
        s_ref, refs = refs[0], refs[1:]
    if kind == "away":
        krylov_ref, heat_in, refs = refs[0], refs[1:8], refs[8:]
    if kind == "mine":
        kk_ref, refs = refs[0], refs[1:]
    out_ref, refs = refs[0], refs[1:]
    if kind == "away":
        kk_ref, heat_out, refs = refs[0], refs[1:3], refs[3:]
    b_scr, w_scr = refs[:2]
    total = refs[2] if finish else out_ref
    step, group = pl.program_id(0), pl.program_id(1)
    width = cols_ref.shape[2]
    span = w_scr.shape[1]
    chunks = span // width
    base = pl.multiple_of(group * group_rows, group_rows)

    @pl.when(group == 0)
    def _():
        for y in range(chunks):
            at = slice(y * width, (y + 1) * width)
            geo = cols_ref[step * chunks + y, 0:16, :].astype(F32)
            wire = cols_ref[step * chunks + y, 16:32, :].astype(F32)
            b_scr[at, :] = jnp.concatenate([geo, geo, geo], axis=0).T.astype(BF16)
            for c in range(3):
                seg = geo[9 + c : 10 + c] + geo[12 + c : 13 + c]
                w_scr[16 * c : 16 * (c + 1), at] = (wire * seg).astype(BF16)

    def rows_at(k, offset):
        return pl.ds(pl.multiple_of(offset + base + k * ROW_TILE, ROW_TILE), ROW_TILE)

    @pl.when(step == 0)
    def _():
        for k in range(group_rows // ROW_TILE):
            if acc_ref is None:
                total[:, rows_at(k, 0)] = jnp.zeros((3 * SECTIONS, ROW_TILE), F32)
            else:
                total[:, rows_at(k, 0)] = acc_ref[:, rows_at(k, row0)]

    sums = {}

    def add(k, at, tile):
        part = jnp.dot(w_scr[:, at], tile, preferred_element_type=F32)
        sums[k] = sums[k] + part if k in sums else part
        if at.stop == span:
            total[:, rows_at(k, 0)] += sums[k]

    held = None
    for k in range(group_rows // ROW_TILE):
        for j in range(0, span, COL_TILE):
            at = slice(j, j + COL_TILE)
            r2 = jnp.dot(b_scr[at, :], a_ref[:, rows_at(k, row0)], preferred_element_type=F32)
            tile = lax.rsqrt(r2).astype(BF16)
            if held is not None:
                add(*held)
            held = (k, at, tile)
    add(*held)

    if finish:

        @pl.when(step == pl.num_programs(0) - 1)
        def _():
            for k in range(group_rows // width):
                here = pl.ds(pl.multiple_of(base + k * width, width), width)
                turned = total[:, here]
                block = group * (group_rows // width) + k
                seg = s_ref[row0 // width + block]
                out_ref[block, 0:16, :] = (
                    turned[0:16] * seg[0:1] + turned[16:32] * seg[1:2] + turned[32:48] * seg[2:3]
                )

        @pl.when((step == 0) & (group == 0))
        def _():
            if kind == "away":
                krylov = krylov_ref[...]
                kk_ref[...] = lax.dot_general(
                    krylov, krylov, NT, precision=HI, preferred_element_type=F32
                )
                heat(*heat_in, *heat_out)
            me = lax.axis_index("row")
            for n in range(out_ref.shape[0]):
                shift, swap = BLOCKS[row0 // width + n]
                owner = (me // 2 + 4 - shift) % 4 * 2 + (me + swap) % 2
                out_ref[n, 16:24, :] = jnp.zeros((8, width), F32)
                out_ref[n, 16:24, 0:64] = kk_ref[pl.ds(pl.multiple_of(owner * 8, 8), 8), :]


def flux_call(kind, cols, a, *more, row0=0, rows, group_rows, step_chunks):
    chunks, _, width = cols.shape
    finish = kind in ("away", "mine")
    whole = pl.BlockSpec(memory_space=pltpu.VMEM)
    scalar = pl.BlockSpec(memory_space=pltpu.SMEM)
    args = [cols, a, *more]
    specs = [whole] * len(args)
    if finish:
        shapes = [jax.ShapeDtypeStruct((rows // width, SECTIONS + 8, width), F32)]
    else:
        shapes = [jax.ShapeDtypeStruct((3 * SECTIONS, rows), F32)]
    if kind == "away":
        specs[-2:] = [scalar] * 2
        shapes += [jax.ShapeDtypeStruct((64, 64), F32)]
        shapes += [jax.ShapeDtypeStruct((1, width), F32)] * 2
    span = step_chunks * width
    scratch = [pltpu.VMEM((span, 48), BF16), pltpu.VMEM((48, span), BF16)]
    if finish:
        scratch.append(pltpu.VMEM((3 * SECTIONS, rows), F32))
    pairs = rows * chunks * width
    out = pl.pallas_call(
        functools.partial(flux_body, kind, row0, group_rows),
        grid=(chunks // step_chunks, rows // group_rows),
        in_specs=specs,
        out_specs=[whole] * len(shapes),
        out_shape=shapes,
        scratch_shapes=scratch,
        compiler_params=pltpu.CompilerParams(vmem_limit_bytes=40 * 2**20),
        cost_estimate=pl.CostEstimate(
            flops=pairs * 2 * 512, bytes_accessed=4 * rows * 128, transcendentals=pairs
        ),
        name="flux",
    )(*args)
    return out if kind == "away" else out[0]


def image_body(sent1, sent3, sent2, mine_ref, swap_ref, rho_ref, amps_ref, krylov_ref, image_ref, stats_ref):
    flux = (sent1[0] + sent3[0] + sent2[0] + mine_ref[1]) + swap_ref[...]
    image = rho_ref[...] * amps_ref[...] + flux[0:16]
    image_ref[...] = image
    kk = flux[16:24, 0:64]
    dot = functools.partial(
        lax.dot_general, dimension_numbers=NT, precision=HI, preferred_element_type=F32
    )
    parts = [
        dot(image, krylov_ref[...]),
        dot(image, image),
        jnp.concatenate([kk[:, 0:32], kk[:, 32:64]], axis=0),
        jnp.zeros((SECTIONS, 16), F32),
    ]
    stats = jnp.concatenate(parts, axis=1)
    for n in range(stats_ref.shape[0]):
        stats_ref[n] = stats


def middle_body(in_ref, out_ref):
    halves = []
    for c in range(2):
        half = in_ref[8 * c]
        for z in range(1, 8):
            half = half + in_ref[8 * c + z]
        halves.append(half)
    lane = lax.broadcasted_iota(jnp.int32, halves[0].shape, 1)
    main = jnp.where(lane < 80, halves[0] + halves[1], halves[0])
    other = halves[1]
    parts = [other[0:8, 80:112], other[8:16, 80:112], jnp.zeros((8, 64), F32)]
    extra = jnp.concatenate(parts, axis=1)
    for n in range(16):
        out_ref[n, 0:16, :] = main
        out_ref[n, 16:24, :] = extra


def end_body(krylov_ref, image_ref, stats_ref, q_ref, hess_ref, chol_ref, kk_scr):
    dot = functools.partial(lax.dot_general, precision=HI, preferred_element_type=F32)
    nn = (((1,), (0,)), ((), ()))
    stats = None
    for x in range(4):
        part = stats_ref[4 * x]
        for y in range(1, 4):
            part = part + stats_ref[4 * x + y]
        kk_scr[16 * x : 16 * x + 8, 0:32] = part[0:8, 80:112]
        kk_scr[16 * x : 16 * x + 8, 32:64] = part[8:16, 80:112]
        kk_scr[16 * x + 8 : 16 * x + 16, :] = part[16:24, 0:64]
        stats = part if stats is None else stats + part
    stats = stats[0:16]
    turned = stats[:, 0:64]
    hess_ref[...] = turned
    kh = dot(turned, kk_scr[...], nn)
    gram = stats[:, 64:80] + dot(kh - 2.0 * turned, turned, NT)
    resid = image_ref[...] - dot(turned, krylov_ref[...], nn)
    row = lax.broadcasted_iota(jnp.int32, gram.shape, 0)
    col = lax.broadcasted_iota(jnp.int32, gram.shape, 1)
    chol = jnp.zeros_like(gram)
    for j in range(SECTIONS):
        column = gram[:, j : j + 1]
        chol = jnp.where(col == j, column, chol)
        ratio = column / gram[j : j + 1, j : j + 1]
        resid = resid - jnp.where(row[:, 0:1] > j, ratio, 0.0) * resid[j : j + 1, :]
        gram = gram - ratio * gram[j : j + 1, :]
    chol = jnp.where(row >= col, chol, 0.0)
    pivot = jnp.where(row == col, chol, 0.0)
    q_ref[...] = resid / jnp.sqrt(jnp.sum(pivot, axis=1, keepdims=True))
    chol_ref[...] = chol / jnp.sqrt(jnp.sum(pivot, axis=0, keepdims=True))


def end_call(krylov, image, stats):
    whole = pl.BlockSpec(memory_space=pltpu.VMEM)
    return pl.pallas_call(
        end_body,
        in_specs=[whole] * 3,
        out_specs=[whole] * 3,
        out_shape=[
            jax.ShapeDtypeStruct(image.shape, F32),
            jax.ShapeDtypeStruct((SECTIONS, krylov.shape[0]), F32),
            jax.ShapeDtypeStruct((SECTIONS, SECTIONS), F32),
        ],
        scratch_shapes=[pltpu.VMEM((64, 64), F32)],
        compiler_params=pltpu.CompilerParams(vmem_limit_bytes=16 * 2**20),
        name="finish",
    )(krylov, image, stats)


def core_swap(value):
    return lax.ppermute(value, "row", [(i, i ^ 1) for i in range(8)])


def shift_x(value, k):
    return lax.ppermute(value, "row", [(i, (i + 2 * k) % 8) for i in range(8)])


def shift_y(value, k):
    return lax.ppermute(value, "col", [(i, (i + 8 * k) % 32) for i in range(32)])


def swap_z(value, k):
    return lax.ppermute(value, "col", [(i, i ^ k) for i in range(32)])


def local(
    strand_layout,
    strand_amperes_panel,
    krylov_vectors,
    strand_kelvin,
    strand_ohmic_value,
    strand_warmer_slot,
    warmer_kelvin_gain,
    strand_region_slot,
    region_threshold_kelvin,
):
    width = strand_kelvin.shape[0]
    own = small_call(
        payload_body, (strand_layout, strand_amperes_panel), [((32, width), BF16)], "payload"
    )[0]
    ys = [shift_y(own, k) for k in (1, 3)]
    pair = jnp.stack([own, core_swap(own)])
    late, pair = lax.optimization_barrier((own, pair))
    others = [shift_x(pair, k) for k in (2, 3, 1)][::-1]
    column = jnp.stack([late] + ys + [shift_y(late, 2)])

    a, seg = small_call(
        rows_body, (*others, pair), [((48, 8 * width), BF16), ((8, 8, width), F32)], "rows"
    )
    count = a.shape[1]
    far = swap_z(column, 4)
    acc = flux_call("first", column[:2], a, rows=count, group_rows=2048, step_chunks=2)
    whole = jnp.concatenate([column, far], axis=0)
    middle = swap_z(whole, 2)
    acc = flux_call("next", whole[2:], a, acc, rows=count, group_rows=1024, step_chunks=6)
    whole = jnp.concatenate([whole, middle], axis=0)
    near = swap_z(whole, 1)
    acc = flux_call("next", middle, a, acc, rows=count, group_rows=1024, step_chunks=8)
    flat = (strand_kelvin, strand_ohmic_value, strand_warmer_slot, strand_region_slot)
    away, kk, rho, joule = flux_call(
        "away", near, a, acc, seg, krylov_vectors, *(v[None] for v in flat), strand_amperes_panel,
        warmer_kelvin_gain, region_threshold_kelvin,
        rows=3072, group_rows=1024, step_chunks=8,
    )
    sent = [shift_x(away[2 * n : 2 * n + 2], -k) for n, k in ((2, 2), (1, 3), (0, 1))][::-1]
    mine = flux_call(
        "mine", near, a, acc, seg, kk, row0=3072, rows=1024, group_rows=1024, step_chunks=8
    )
    swapped = core_swap(sent[0][1] + sent[1][1] + sent[2][1] + mine[0])

    image, stats = small_call(
        image_body,
        (*sent, mine, swapped, rho, strand_amperes_panel, krylov_vectors),
        [((SECTIONS, width), F32), ((16, SECTIONS, 128), F32)],
        "image",
    )
    stats = lax.all_to_all(stats, ("row", "col"), 0, 0, axis_index_groups=CORE_Z)
    stats = small_call(middle_body, (stats,), [((16, 24, 128), F32)], "middle")[0]
    stats = lax.all_to_all(stats, ("row", "col"), 0, 0, axis_index_groups=X_Y)
    q_next, hess, chol = end_call(krylov_vectors, image, stats)
    return (q_next, hess.T, chol, joule[0])


def solution(mesh):
    return jax.shard_map(
        local,
        mesh=mesh,
        in_specs=(
            P(None, ("row", "col")),
            P(None, ("row", "col")),
            P(None, ("row", "col")),
            P(("row", "col")),
            P(("row", "col")),
            P(("row", "col")),
            P(),
            P(("row", "col")),
            P(),
        ),
        out_specs=(P(None, ("row", "col")), P(), P(), P(("row", "col"))),
        check_vma=False,
    )
```

```python
import functools

import jax
import jax.numpy as jnp
from jax import lax
from jax.experimental import pallas as pl
from jax.experimental.pallas import tpu as pltpu
from jax.sharding import PartitionSpec as P

HI = lax.Precision.HIGHEST
F32 = jnp.float32
BF16 = jnp.bfloat16
NT = (((1,), (1,)), ((), ()))
SECTIONS = 16
ROW_TILE = 1024
COL_TILE = 256
CORE_Z = [
    [(2 * x + c) * 32 + 8 * y + z for c in range(2) for z in range(8)]
    for x in range(4)
    for y in range(4)
]
X_Y = [
    [(2 * x + c) * 32 + 8 * y + z for x in range(4) for y in range(4)]
    for c in range(2)
    for z in range(8)
]
BLOCKS = ((1, 0), (1, 1), (3, 0), (3, 1), (2, 0), (2, 1), (0, 1), (0, 0))


def small_call(body, args, shapes, name):
    whole = pl.BlockSpec(memory_space=pltpu.VMEM)
    return pl.pallas_call(
        body,
        in_specs=[whole] * len(args),
        out_specs=[whole] * len(shapes),
        out_shape=[jax.ShapeDtypeStruct(shape, dtype) for shape, dtype in shapes],
        compiler_params=pltpu.CompilerParams(vmem_limit_bytes=16 * 2**20),
        name=name,
    )(*args)


def pieces(value, count):
    out = []
    for _ in range(count):
        piece = value.astype(BF16).astype(F32)
        out.append(piece)
        value = value - piece
    return out


def payload_body(layout_ref, amps_ref, out_ref):
    layout = layout_ref[...]
    high, low = pieces(layout[0:3] - 0.5, 2)
    centre = high + low
    square = centre * centre
    soft = square[0:1] + square[1:2] + square[2:3] + layout[6:7] * layout[6:7]
    parts = [high, low, *pieces(soft, 3), *pieces(layout[3:6], 2), jnp.ones_like(soft)]
    out_ref[0:16, :] = jnp.concatenate(parts, axis=0).astype(BF16)
    out_ref[16:32, :] = amps_ref[...].astype(BF16)


def heat(kelvin_ref, ohmic_ref, warmer_ref, region_ref, amps_ref, gain_ref, limit_ref, rho_ref, joule_ref):
    def entries(ids, table_ref):
        out = jnp.zeros(ids.shape, F32)
        table = table_ref[...]
        for level in range(table.shape[1]):
            out = jnp.where(ids == level, table[:, level : level + 1], out)
        return out

    warm = entries(warmer_ref[...], gain_ref)
    limit = entries(region_ref[...], limit_ref)
    rho = ohmic_ref[...] / (1.0 + jnp.exp(limit - (kelvin_ref[...] + warm)))
    amps = amps_ref[...]
    rho_ref[...] = rho
    joule_ref[...] = rho * jnp.mean(amps * amps, axis=0, keepdims=True)


def rows_body(x1_ref, x3_ref, x2_ref, pair_ref, *refs):
    a_ref, s_ref = refs[7:9]
    heat(*refs[:7], *refs[9:])
    blocks = [ref[n] for ref in (x1_ref, x3_ref, x2_ref) for n in range(2)]
    blocks += [pair_ref[1], pair_ref[0]]
    width = s_ref.shape[2]
    for n, block in enumerate(blocks):
        geo = block[0:16].astype(F32)
        high, low = -2.0 * geo[0:3], -2.0 * geo[3:6]
        zero = jnp.zeros((15, width), F32)
        one = jnp.ones((3, width), F32)
        parts = [high, high, one, zero[0:6], geo[6:7]]
        parts += [low, low, zero[0:9], geo[7:8], zero, geo[8:9]]
        a_ref[:, n * width : (n + 1) * width] = jnp.concatenate(parts, axis=0).astype(BF16)
        s_ref[n] = jnp.concatenate([geo[9:12] + geo[12:15], zero[0:5]], axis=0)


def flux_body(kind, row0, group_rows, cols_ref, a_ref, *refs):
    finish = kind in ("away", "mine")
    acc_ref = None
    if kind != "first":
        acc_ref, refs = refs[0], refs[1:]
    if finish:
        s_ref, refs = refs[0], refs[1:]
    if kind == "away":
        krylov_ref, refs = refs[0], refs[1:]
    if kind == "mine":
        kk_ref, refs = refs[0], refs[1:]
    out_ref, refs = refs[0], refs[1:]
    if kind == "away":
        kk_ref, refs = refs[0], refs[1:]
    b_scr, w_scr = refs[:2]
    total = refs[2] if finish else out_ref
    step, group = pl.program_id(0), pl.program_id(1)
    width = cols_ref.shape[2]
    span = w_scr.shape[1]
    chunks = span // width
    base = pl.multiple_of(group * group_rows, group_rows)

    @pl.when(group == 0)
    def _():
        for y in range(chunks):
            at = slice(y * width, (y + 1) * width)
            geo = cols_ref[step * chunks + y, 0:16, :].astype(F32)
            wire = cols_ref[step * chunks + y, 16:32, :].astype(F32)
            b_scr[at, :] = jnp.concatenate([geo, geo, geo], axis=0).T.astype(BF16)
            for c in range(3):
                seg = geo[9 + c : 10 + c] + geo[12 + c : 13 + c]
                w_scr[16 * c : 16 * (c + 1), at] = (wire * seg).astype(BF16)

    def rows_at(k, offset):
        return pl.ds(pl.multiple_of(offset + base + k * ROW_TILE, ROW_TILE), ROW_TILE)

    @pl.when(step == 0)
    def _():
        for k in range(group_rows // ROW_TILE):
            if acc_ref is None:
                total[:, rows_at(k, 0)] = jnp.zeros((3 * SECTIONS, ROW_TILE), F32)
            else:
                total[:, rows_at(k, 0)] = acc_ref[:, rows_at(k, row0)]

    sums = {}

    def add(k, at, tile):
        part = jnp.dot(w_scr[:, at], tile, preferred_element_type=F32)
        sums[k] = sums[k] + part if k in sums else part
        if at.stop == span:
            total[:, rows_at(k, 0)] += sums[k]

    held = None
    for k in range(group_rows // ROW_TILE):
        for j in range(0, span, COL_TILE):
            at = slice(j, j + COL_TILE)
            r2 = jnp.dot(b_scr[at, :], a_ref[:, rows_at(k, row0)], preferred_element_type=F32)
            tile = lax.rsqrt(r2).astype(BF16)
            if held is not None:
                add(*held)
            held = (k, at, tile)
    add(*held)

    if finish:

        @pl.when(step == pl.num_programs(0) - 1)
        def _():
            for k in range(group_rows // width):
                here = pl.ds(pl.multiple_of(base + k * width, width), width)
                turned = total[:, here]
                block = group * (group_rows // width) + k
                seg = s_ref[row0 // width + block]
                out_ref[block, 0:16, :] = (
                    turned[0:16] * seg[0:1] + turned[16:32] * seg[1:2] + turned[32:48] * seg[2:3]
                )

        @pl.when((step == 0) & (group == 0))
        def _():
            if kind == "away":
                krylov = krylov_ref[...]
                kk_ref[...] = lax.dot_general(
                    krylov, krylov, NT, precision=HI, preferred_element_type=F32
                )
            me = lax.axis_index("row")
            for n in range(out_ref.shape[0]):
                shift, swap = BLOCKS[row0 // width + n]
                owner = (me // 2 + 4 - shift) % 4 * 2 + (me + swap) % 2
                out_ref[n, 16:24, :] = jnp.zeros((8, width), F32)
                out_ref[n, 16:24, 0:64] = kk_ref[pl.ds(pl.multiple_of(owner * 8, 8), 8), :]


def flux_call(kind, cols, a, *more, row0=0, rows, group_rows, step_chunks):
    chunks, _, width = cols.shape
    finish = kind in ("away", "mine")
    whole = pl.BlockSpec(memory_space=pltpu.VMEM)
    args = [cols, a, *more]
    specs = [whole] * len(args)
    if finish:
        shapes = [jax.ShapeDtypeStruct((rows // width, SECTIONS + 8, width), F32)]
    else:
        shapes = [jax.ShapeDtypeStruct((3 * SECTIONS, rows), F32)]
    if kind == "away":
        shapes.append(jax.ShapeDtypeStruct((64, 64), F32))
    span = step_chunks * width
    scratch = [pltpu.VMEM((span, 48), BF16), pltpu.VMEM((48, span), BF16)]
    if finish:
        scratch.append(pltpu.VMEM((3 * SECTIONS, rows), F32))
    pairs = rows * chunks * width
    out = pl.pallas_call(
        functools.partial(flux_body, kind, row0, group_rows),
        grid=(chunks // step_chunks, rows // group_rows),
        in_specs=specs,
        out_specs=[whole] * len(shapes),
        out_shape=shapes,
        scratch_shapes=scratch,
        compiler_params=pltpu.CompilerParams(vmem_limit_bytes=40 * 2**20),
        cost_estimate=pl.CostEstimate(
            flops=pairs * 2 * 512, bytes_accessed=4 * rows * 128, transcendentals=pairs
        ),
        name="flux",
    )(*args)
    return out if kind == "away" else out[0]


def image_body(sent1, sent3, sent2, mine_ref, swap_ref, rho_ref, amps_ref, krylov_ref, image_ref, stats_ref):
    flux = (sent1[0] + sent3[0] + sent2[0] + mine_ref[1]) + swap_ref[...]
    image = rho_ref[...] * amps_ref[...] + flux[0:16]
    image_ref[...] = image
    kk = flux[16:24, 0:64]
    dot = functools.partial(
        lax.dot_general, dimension_numbers=NT, precision=HI, preferred_element_type=F32
    )
    parts = [
        dot(image, krylov_ref[...]),
        dot(image, image),
        jnp.concatenate([kk[:, 0:32], kk[:, 32:64]], axis=0),
        jnp.zeros((SECTIONS, 16), F32),
    ]
    stats = jnp.concatenate(parts, axis=1)
    for n in range(stats_ref.shape[0]):
        stats_ref[n] = stats


def middle_body(in_ref, out_ref):
    halves = []
    for c in range(2):
        half = in_ref[8 * c]
        for z in range(1, 8):
            half = half + in_ref[8 * c + z]
        halves.append(half)
    lane = lax.broadcasted_iota(jnp.int32, halves[0].shape, 1)
    main = jnp.where(lane < 80, halves[0] + halves[1], halves[0])
    other = halves[1]
    parts = [other[0:8, 80:112], other[8:16, 80:112], jnp.zeros((8, 64), F32)]
    extra = jnp.concatenate(parts, axis=1)
    for n in range(16):
        out_ref[n, 0:16, :] = main
        out_ref[n, 16:24, :] = extra


def end_body(krylov_ref, image_ref, stats_ref, q_ref, hess_ref, chol_ref, kk_scr):
    dot = functools.partial(lax.dot_general, precision=HI, preferred_element_type=F32)
    nn = (((1,), (0,)), ((), ()))
    stats = None
    for x in range(4):
        part = stats_ref[4 * x]
        for y in range(1, 4):
            part = part + stats_ref[4 * x + y]
        kk_scr[16 * x : 16 * x + 8, 0:32] = part[0:8, 80:112]
        kk_scr[16 * x : 16 * x + 8, 32:64] = part[8:16, 80:112]
        kk_scr[16 * x + 8 : 16 * x + 16, :] = part[16:24, 0:64]
        stats = part if stats is None else stats + part
    stats = stats[0:16]
    turned = stats[:, 0:64]
    hess_ref[...] = turned
    kh = dot(turned, kk_scr[...], nn)
    gram = stats[:, 64:80] + dot(kh - 2.0 * turned, turned, NT)
    resid = image_ref[...] - dot(turned, krylov_ref[...], nn)
    row = lax.broadcasted_iota(jnp.int32, gram.shape, 0)
    col = lax.broadcasted_iota(jnp.int32, gram.shape, 1)
    chol = jnp.zeros_like(gram)
    for j in range(SECTIONS):
        column = gram[:, j : j + 1]
        chol = jnp.where(col == j, column, chol)
        ratio = column / gram[j : j + 1, j : j + 1]
        resid = resid - jnp.where(row[:, 0:1] > j, ratio, 0.0) * resid[j : j + 1, :]
        gram = gram - ratio * gram[j : j + 1, :]
    chol = jnp.where(row >= col, chol, 0.0)
    pivot = jnp.where(row == col, chol, 0.0)
    q_ref[...] = resid / jnp.sqrt(jnp.sum(pivot, axis=1, keepdims=True))
    chol_ref[...] = chol / jnp.sqrt(jnp.sum(pivot, axis=0, keepdims=True))


def end_call(krylov, image, stats):
    whole = pl.BlockSpec(memory_space=pltpu.VMEM)
    return pl.pallas_call(
        end_body,
        in_specs=[whole] * 3,
        out_specs=[whole] * 3,
        out_shape=[
            jax.ShapeDtypeStruct(image.shape, F32),
            jax.ShapeDtypeStruct((SECTIONS, krylov.shape[0]), F32),
            jax.ShapeDtypeStruct((SECTIONS, SECTIONS), F32),
        ],
        scratch_shapes=[pltpu.VMEM((64, 64), F32)],
        compiler_params=pltpu.CompilerParams(vmem_limit_bytes=16 * 2**20),
        name="finish",
    )(krylov, image, stats)


def core_swap(value):
    return lax.ppermute(value, "row", [(i, i ^ 1) for i in range(8)])


def shift_x(value, k):
    return lax.ppermute(value, "row", [(i, (i + 2 * k) % 8) for i in range(8)])


def shift_y(value, k):
    return lax.ppermute(value, "col", [(i, (i + 8 * k) % 32) for i in range(32)])


def swap_z(value, k):
    return lax.ppermute(value, "col", [(i, i ^ k) for i in range(32)])


def local(
    strand_layout,
    strand_amperes_panel,
    krylov_vectors,
    strand_kelvin,
    strand_ohmic_value,
    strand_warmer_slot,
    warmer_kelvin_gain,
    strand_region_slot,
    region_threshold_kelvin,
):
    width = strand_kelvin.shape[0]
    own = small_call(
        payload_body, (strand_layout, strand_amperes_panel), [((32, width), BF16)], "payload"
    )[0]
    ys = [shift_y(own, k) for k in (1, 3)]
    pair = jnp.stack([own, core_swap(own)])
    late, pair = lax.optimization_barrier((own, pair))
    others = [shift_x(pair, k) for k in (2, 3, 1)][::-1]
    column = jnp.stack([late] + ys + [shift_y(late, 2)])

    flat = (strand_kelvin, strand_ohmic_value, strand_warmer_slot, strand_region_slot)
    a, seg, rho, joule = small_call(
        rows_body,
        (*others, pair, *(v[None] for v in flat), strand_amperes_panel, warmer_kelvin_gain[None],
         region_threshold_kelvin[None]),
        [((48, 8 * width), BF16), ((8, 8, width), F32), ((1, width), F32), ((1, width), F32)],
        "rows",
    )
    count = a.shape[1]
    far = swap_z(column, 4)
    acc = flux_call("first", column[:2], a, rows=count, group_rows=2048, step_chunks=2)
    whole = jnp.concatenate([column, far], axis=0)
    middle = swap_z(whole, 2)
    acc = flux_call("next", whole[2:], a, acc, rows=count, group_rows=1024, step_chunks=6)
    whole = jnp.concatenate([whole, middle], axis=0)
    near = swap_z(whole, 1)
    acc = flux_call("next", middle, a, acc, rows=count, group_rows=1024, step_chunks=8)
    away, kk = flux_call(
        "away", near, a, acc, seg, krylov_vectors, rows=3072, group_rows=1024, step_chunks=16
    )
    sent = [shift_x(away[2 * n : 2 * n + 2], -k) for n, k in ((2, 2), (1, 3), (0, 1))][::-1]
    mine = flux_call(
        "mine", near, a, acc, seg, kk, row0=3072, rows=1024, group_rows=1024, step_chunks=16
    )
    swapped = core_swap(sent[0][1] + sent[1][1] + sent[2][1] + mine[0])

    image, stats = small_call(
        image_body,
        (*sent, mine, swapped, rho, strand_amperes_panel, krylov_vectors),
        [((SECTIONS, width), F32), ((16, SECTIONS, 128), F32)],
        "image",
    )
    stats = lax.all_to_all(stats, ("row", "col"), 0, 0, axis_index_groups=CORE_Z)
    stats = small_call(middle_body, (stats,), [((16, 24, 128), F32)], "middle")[0]
    stats = lax.all_to_all(stats, ("row", "col"), 0, 0, axis_index_groups=X_Y)
    q_next, hess, chol = end_call(krylov_vectors, image, stats)
    return (q_next, hess.T, chol, joule[0])


def solution(mesh):
    return jax.shard_map(
        local,
        mesh=mesh,
        in_specs=(
            P(None, ("row", "col")),
            P(None, ("row", "col")),
            P(None, ("row", "col")),
            P(("row", "col")),
            P(("row", "col")),
            P(("row", "col")),
            P(),
            P(("row", "col")),
            P(),
        ),
        out_specs=(P(None, ("row", "col")), P(), P(), P(("row", "col"))),
        check_vma=False,
    )
```

```python
import functools

import jax
import jax.numpy as jnp
from jax import lax
from jax.experimental import pallas as pl
from jax.experimental.pallas import tpu as pltpu
from jax.sharding import PartitionSpec as P

HI = lax.Precision.HIGHEST
F32 = jnp.float32
BF16 = jnp.bfloat16
NT = (((1,), (1,)), ((), ()))
SECTIONS = 16
ROW_TILE = 1024
COL_TILE = 256
CORE_Z = [
    [(2 * x + c) * 32 + 8 * y + z for c in range(2) for z in range(8)]
    for x in range(4)
    for y in range(4)
]
X_Y = [
    [(2 * x + c) * 32 + 8 * y + z for x in range(4) for y in range(4)]
    for c in range(2)
    for z in range(8)
]
BLOCKS = ((1, 0), (1, 1), (3, 0), (3, 1), (2, 0), (2, 1), (0, 1), (0, 0))


def small_call(body, args, shapes, name):
    whole = pl.BlockSpec(memory_space=pltpu.VMEM)
    return pl.pallas_call(
        body,
        in_specs=[whole] * len(args),
        out_specs=[whole] * len(shapes),
        out_shape=[jax.ShapeDtypeStruct(shape, dtype) for shape, dtype in shapes],
        compiler_params=pltpu.CompilerParams(vmem_limit_bytes=16 * 2**20),
        name=name,
    )(*args)


def pieces(value, count):
    out = []
    for _ in range(count):
        piece = value.astype(BF16).astype(F32)
        out.append(piece)
        value = value - piece
    return out


def payload_body(layout_ref, amps_ref, out_ref, power_ref):
    layout = layout_ref[...]
    high, low = pieces(layout[0:3] - 0.5, 2)
    centre = high + low
    square = centre * centre
    soft = square[0:1] + square[1:2] + square[2:3] + layout[6:7] * layout[6:7]
    parts = [high, low, *pieces(soft, 3), *pieces(layout[3:6], 2), jnp.ones_like(soft)]
    out_ref[0:16, :] = jnp.concatenate(parts, axis=0).astype(BF16)
    amps = amps_ref[...]
    out_ref[16:32, :] = amps.astype(BF16)
    power_ref[...] = jnp.mean(amps * amps, axis=0, keepdims=True)


def heat(kelvin_ref, ohmic_ref, warmer_ref, region_ref, power_ref, gain_ref, limit_ref, rho_ref, joule_ref):
    def entries(ids, table_ref):
        out = jnp.zeros(ids.shape, F32)
        table = table_ref[...]
        for level in range(table.shape[1]):
            out = jnp.where(ids == level, table[:, level : level + 1], out)
        return out

    warm = entries(warmer_ref[...], gain_ref)
    limit = entries(region_ref[...], limit_ref)
    rho = ohmic_ref[...] / (1.0 + jnp.exp(limit - (kelvin_ref[...] + warm)))
    rho_ref[...] = rho
    joule_ref[...] = rho * power_ref[...]


def rows_body(x1_ref, x3_ref, x2_ref, pair_ref, *refs):
    a_ref, s_ref = refs[7:9]
    heat(*refs[:7], *refs[9:])
    blocks = [ref[n] for ref in (x1_ref, x3_ref, x2_ref) for n in range(2)]
    blocks += [pair_ref[1], pair_ref[0]]
    width = s_ref.shape[2]
    for n, block in enumerate(blocks):
        geo = block[0:16].astype(F32)
        high, low = -2.0 * geo[0:3], -2.0 * geo[3:6]
        zero = jnp.zeros((15, width), F32)
        one = jnp.ones((3, width), F32)
        parts = [high, high, one, zero[0:6], geo[6:7]]
        parts += [low, low, zero[0:9], geo[7:8], zero, geo[8:9]]
        a_ref[:, n * width : (n + 1) * width] = jnp.concatenate(parts, axis=0).astype(BF16)
        s_ref[n] = jnp.concatenate([geo[9:12] + geo[12:15], zero[0:5]], axis=0)


def flux_body(kind, row0, group_rows, cols_ref, a_ref, *refs):
    finish = kind in ("away", "mine")
    acc_ref = None
    if kind != "first":
        acc_ref, refs = refs[0], refs[1:]
    if finish:
        s_ref, refs = refs[0], refs[1:]
    if kind == "away":
        krylov_ref, refs = refs[0], refs[1:]
    if kind == "mine":
        kk_ref, refs = refs[0], refs[1:]
    out_ref, refs = refs[0], refs[1:]
    if kind == "away":
        kk_ref, refs = refs[0], refs[1:]
    b_scr, w_scr = refs[:2]
    total = refs[2] if finish else out_ref
    step, group = pl.program_id(0), pl.program_id(1)
    width = cols_ref.shape[2]
    span = w_scr.shape[1]
    chunks = span // width
    base = pl.multiple_of(group * group_rows, group_rows)

    @pl.when(group == 0)
    def _():
        for y in range(chunks):
            at = slice(y * width, (y + 1) * width)
            geo = cols_ref[step * chunks + y, 0:16, :].astype(F32)
            wire = cols_ref[step * chunks + y, 16:32, :].astype(F32)
            b_scr[at, :] = jnp.concatenate([geo, geo, geo], axis=0).T.astype(BF16)
            for c in range(3):
                seg = geo[9 + c : 10 + c] + geo[12 + c : 13 + c]
                w_scr[16 * c : 16 * (c + 1), at] = (wire * seg).astype(BF16)

    def rows_at(k, offset):
        return pl.ds(pl.multiple_of(offset + base + k * ROW_TILE, ROW_TILE), ROW_TILE)

    @pl.when(step == 0)
    def _():
        for k in range(group_rows // ROW_TILE):
            if acc_ref is None:
                total[:, rows_at(k, 0)] = jnp.zeros((3 * SECTIONS, ROW_TILE), F32)
            else:
                total[:, rows_at(k, 0)] = acc_ref[:, rows_at(k, row0)]

    sums = {}

    def add(k, at, tile):
        part = jnp.dot(w_scr[:, at], tile, preferred_element_type=F32)
        sums[k] = sums[k] + part if k in sums else part
        if at.stop == span:
            total[:, rows_at(k, 0)] += sums[k]

    held = None
    for k in range(group_rows // ROW_TILE):
        for j in range(0, span, COL_TILE):
            at = slice(j, j + COL_TILE)
            r2 = jnp.dot(b_scr[at, :], a_ref[:, rows_at(k, row0)], preferred_element_type=F32)
            tile = lax.rsqrt(r2).astype(BF16)
            if held is not None:
                add(*held)
            held = (k, at, tile)
    add(*held)

    if finish:

        @pl.when(step == pl.num_programs(0) - 1)
        def _():
            for k in range(group_rows // width):
                here = pl.ds(pl.multiple_of(base + k * width, width), width)
                turned = total[:, here]
                block = group * (group_rows // width) + k
                seg = s_ref[row0 // width + block]
                out_ref[block, 0:16, :] = (
                    turned[0:16] * seg[0:1] + turned[16:32] * seg[1:2] + turned[32:48] * seg[2:3]
                )

        @pl.when((step == 0) & (group == 0))
        def _():
            if kind == "away":
                krylov = krylov_ref[...]
                kk_ref[...] = lax.dot_general(
                    krylov, krylov, NT, precision=HI, preferred_element_type=F32
                )
            me = lax.axis_index("row")
            for n in range(out_ref.shape[0]):
                shift, swap = BLOCKS[row0 // width + n]
                owner = (me // 2 + 4 - shift) % 4 * 2 + (me + swap) % 2
                out_ref[n, 16:24, :] = jnp.zeros((8, width), F32)
                out_ref[n, 16:24, 0:64] = kk_ref[pl.ds(pl.multiple_of(owner * 8, 8), 8), :]


def flux_call(kind, cols, a, *more, row0=0, rows, group_rows, step_chunks):
    chunks, _, width = cols.shape
    finish = kind in ("away", "mine")
    whole = pl.BlockSpec(memory_space=pltpu.VMEM)
    args = [cols, a, *more]
    specs = [whole] * len(args)
    if finish:
        shapes = [jax.ShapeDtypeStruct((rows // width, SECTIONS + 8, width), F32)]
    else:
        shapes = [jax.ShapeDtypeStruct((3 * SECTIONS, rows), F32)]
    if kind == "away":
        shapes.append(jax.ShapeDtypeStruct((64, 64), F32))
    span = step_chunks * width
    scratch = [pltpu.VMEM((span, 48), BF16), pltpu.VMEM((48, span), BF16)]
    if finish:
        scratch.append(pltpu.VMEM((3 * SECTIONS, rows), F32))
    pairs = rows * chunks * width
    out = pl.pallas_call(
        functools.partial(flux_body, kind, row0, group_rows),
        grid=(chunks // step_chunks, rows // group_rows),
        in_specs=specs,
        out_specs=[whole] * len(shapes),
        out_shape=shapes,
        scratch_shapes=scratch,
        compiler_params=pltpu.CompilerParams(vmem_limit_bytes=40 * 2**20),
        cost_estimate=pl.CostEstimate(
            flops=pairs * 2 * 512, bytes_accessed=4 * rows * 128, transcendentals=pairs
        ),
        name="flux",
    )(*args)
    return out if kind == "away" else out[0]


def image_body(sent1, sent3, sent2, mine_ref, swap_ref, rho_ref, amps_ref, krylov_ref, image_ref, stats_ref):
    flux = (sent1[0] + sent3[0] + sent2[0] + mine_ref[1]) + swap_ref[...]
    image = rho_ref[...] * amps_ref[...] + flux[0:16]
    image_ref[...] = image
    kk = flux[16:24, 0:64]
    dot = functools.partial(
        lax.dot_general, dimension_numbers=NT, precision=HI, preferred_element_type=F32
    )
    parts = [
        dot(image, krylov_ref[...]),
        dot(image, image),
        jnp.concatenate([kk[:, 0:32], kk[:, 32:64]], axis=0),
        jnp.zeros((SECTIONS, 16), F32),
    ]
    stats = jnp.concatenate(parts, axis=1)
    for n in range(stats_ref.shape[0]):
        stats_ref[n] = stats


def middle_body(in_ref, out_ref):
    halves = []
    for c in range(2):
        half = in_ref[8 * c]
        for z in range(1, 8):
            half = half + in_ref[8 * c + z]
        halves.append(half)
    lane = lax.broadcasted_iota(jnp.int32, halves[0].shape, 1)
    main = jnp.where(lane < 80, halves[0] + halves[1], halves[0])
    other = halves[1]
    parts = [other[0:8, 80:112], other[8:16, 80:112], jnp.zeros((8, 64), F32)]
    extra = jnp.concatenate(parts, axis=1)
    for n in range(16):
        out_ref[n, 0:16, :] = main
        out_ref[n, 16:24, :] = extra


def end_body(krylov_ref, image_ref, stats_ref, q_ref, hess_ref, chol_ref, kk_scr):
    dot = functools.partial(lax.dot_general, precision=HI, preferred_element_type=F32)
    nn = (((1,), (0,)), ((), ()))
    stats = None
    for x in range(4):
        part = stats_ref[4 * x]
        for y in range(1, 4):
            part = part + stats_ref[4 * x + y]
        kk_scr[16 * x : 16 * x + 8, 0:32] = part[0:8, 80:112]
        kk_scr[16 * x : 16 * x + 8, 32:64] = part[8:16, 80:112]
        kk_scr[16 * x + 8 : 16 * x + 16, :] = part[16:24, 0:64]
        stats = part if stats is None else stats + part
    stats = stats[0:16]
    turned = stats[:, 0:64]
    hess_ref[...] = turned
    kh = dot(turned, kk_scr[...], nn)
    gram = stats[:, 64:80] + dot(kh - 2.0 * turned, turned, NT)
    resid = image_ref[...] - dot(turned, krylov_ref[...], nn)
    row = lax.broadcasted_iota(jnp.int32, gram.shape, 0)
    col = lax.broadcasted_iota(jnp.int32, gram.shape, 1)
    chol = jnp.zeros_like(gram)
    for j in range(SECTIONS):
        column = gram[:, j : j + 1]
        chol = jnp.where(col == j, column, chol)
        ratio = column / gram[j : j + 1, j : j + 1]
        resid = resid - jnp.where(row[:, 0:1] > j, ratio, 0.0) * resid[j : j + 1, :]
        gram = gram - ratio * gram[j : j + 1, :]
    chol = jnp.where(row >= col, chol, 0.0)
    pivot = jnp.where(row == col, chol, 0.0)
    q_ref[...] = resid / jnp.sqrt(jnp.sum(pivot, axis=1, keepdims=True))
    chol_ref[...] = chol / jnp.sqrt(jnp.sum(pivot, axis=0, keepdims=True))


def end_call(krylov, image, stats):
    whole = pl.BlockSpec(memory_space=pltpu.VMEM)
    return pl.pallas_call(
        end_body,
        in_specs=[whole] * 3,
        out_specs=[whole] * 3,
        out_shape=[
            jax.ShapeDtypeStruct(image.shape, F32),
            jax.ShapeDtypeStruct((SECTIONS, krylov.shape[0]), F32),
            jax.ShapeDtypeStruct((SECTIONS, SECTIONS), F32),
        ],
        scratch_shapes=[pltpu.VMEM((64, 64), F32)],
        compiler_params=pltpu.CompilerParams(vmem_limit_bytes=16 * 2**20),
        name="finish",
    )(krylov, image, stats)


def core_swap(value):
    return lax.ppermute(value, "row", [(i, i ^ 1) for i in range(8)])


def shift_x(value, k):
    return lax.ppermute(value, "row", [(i, (i + 2 * k) % 8) for i in range(8)])


def shift_y(value, k):
    return lax.ppermute(value, "col", [(i, (i + 8 * k) % 32) for i in range(32)])


def swap_z(value, k):
    return lax.ppermute(value, "col", [(i, i ^ k) for i in range(32)])


def shift_z(value, k):
    return lax.ppermute(value, "col", [(i, i // 8 * 8 + (i + k) % 8) for i in range(32)])


def local(
    strand_layout,
    strand_amperes_panel,
    krylov_vectors,
    strand_kelvin,
    strand_ohmic_value,
    strand_warmer_slot,
    warmer_kelvin_gain,
    strand_region_slot,
    region_threshold_kelvin,
):
    width = strand_kelvin.shape[0]
    own, power = small_call(
        payload_body,
        (strand_layout, strand_amperes_panel),
        [((32, width), BF16), ((1, width), F32)],
        "payload",
    )
    ys = [shift_y(own, k) for k in (1, 3)]
    pair = jnp.stack([own, core_swap(own)])
    late, pair = lax.optimization_barrier((own, pair))
    others = [shift_x(pair, k) for k in (2, 3, 1)][::-1]
    column = jnp.stack([late] + ys + [shift_y(late, 2)])

    flat = (strand_kelvin, strand_ohmic_value, strand_warmer_slot, strand_region_slot)
    a, seg, rho, joule = small_call(
        rows_body,
        (*others, pair, *(v[None] for v in flat), power, warmer_kelvin_gain[None],
         region_threshold_kelvin[None]),
        [((48, 8 * width), BF16), ((8, 8, width), F32), ((1, width), F32), ((1, width), F32)],
        "rows",
    )
    count = a.shape[1]
    far = swap_z(column, 4)
    acc = flux_call("first", column[:2], a, rows=count, group_rows=4096, step_chunks=2)
    whole = jnp.concatenate([column, far], axis=0)
    late, acc = lax.optimization_barrier((column, acc))
    middle = jnp.concatenate([shift_z(late, 2), shift_z(late, -2)], axis=0)
    acc = flux_call("next", whole[2:], a, acc, rows=count, group_rows=2048, step_chunks=6)
    whole = jnp.concatenate([whole, middle], axis=0)
    near = swap_z(whole, 1)
    acc = flux_call("next", middle, a, acc, rows=count, group_rows=2048, step_chunks=8)
    away, kk = flux_call(
        "away", near, a, acc, seg, krylov_vectors, rows=3072, group_rows=1024, step_chunks=16
    )
    sent = [shift_x(away[2 * n : 2 * n + 2], -k) for n, k in ((2, 2), (1, 3), (0, 1))][::-1]
    mine = flux_call(
        "mine", near, a, acc, seg, kk, row0=3072, rows=1024, group_rows=1024, step_chunks=16
    )
    swapped = core_swap(sent[0][1] + sent[1][1] + sent[2][1] + mine[0])

    image, stats = small_call(
        image_body,
        (*sent, mine, swapped, rho, strand_amperes_panel, krylov_vectors),
        [((SECTIONS, width), F32), ((16, SECTIONS, 128), F32)],
        "image",
    )
    stats = lax.all_to_all(stats, ("row", "col"), 0, 0, axis_index_groups=CORE_Z)
    stats = small_call(middle_body, (stats,), [((16, 24, 128), F32)], "middle")[0]
    stats = lax.all_to_all(stats, ("row", "col"), 0, 0, axis_index_groups=X_Y)
    q_next, hess, chol = end_call(krylov_vectors, image, stats)
    return (q_next, hess.T, chol, joule[0])


def solution(mesh):
    return jax.shard_map(
        local,
        mesh=mesh,
        in_specs=(
            P(None, ("row", "col")),
            P(None, ("row", "col")),
            P(None, ("row", "col")),
            P(("row", "col")),
            P(("row", "col")),
            P(("row", "col")),
            P(),
            P(("row", "col")),
            P(),
        ),
        out_specs=(P(None, ("row", "col")), P(), P(), P(("row", "col"))),
        check_vma=False,
    )
```
